128 devices in a mesh: row: 16 (over z, x), col: 8 (over y, core).
Axes of the slice: x: 4, y: 4, z: 4, core: 2. Of those that a mesh axis runs over, the one named last changes fastest.
Arguments:
- resid: bfloat16 [8192, 6144], P('row', 'col'), may hold values from -30 to 30
- attn: bfloat16 [8192, 6144], P('row', 'col'), may hold values from -7 to 7
- attn_tangent: bfloat16 [8192, 6144], P('row', 'col'), may hold values from -7 to 7
- probe: int32 [8192, 6144], P('row', 'col'), may hold values from -1 to 1, as said below
- norm_gain: float32 [6144], P('col'), may hold values from 0.1 to 1.9
- gate_weight: bfloat16 [6144, 8192], P('row', 'col'), may hold values from -0.078125 to 0.078125
- up_weight: bfloat16 [6144, 8192], P('row', 'col'), may hold values from -0.078125 to 0.078125
Outputs:
- state: bfloat16 [8192, 6144], P('row', 'col')
- state_tangent: bfloat16 [8192, 6144], P('row', 'col')
- hidden: bfloat16 [8192, 8192], P('row', 'col')
- hidden_tangent: bfloat16 [8192, 8192], P('row', 'col')
The draws below stay inside these ranges and needn't reach their ends.
Inputs may be any that keep to these rules, and one draw needn't show every extreme that they name: `probe`: each entry is -1 or +1.
All inputs are finite; a program needn't handle non-finite values.
Results may differ from the reference program's by a relative error of at most 0.0078.
Values may be sent and summed in bfloat16 or wider, within the bound.
A program may use at most 512 MiB of HBM per device.

```python
import math
import jax
import jax.numpy as jnp
from jax import lax

D = 6144
FF = 8192
TOKENS = 8192


def common_normal(key):
    return jnp.clip(jax.random.normal(key, (TOKENS, D), jnp.float32), -5.0, 5.0)


def draw_resid(key, part):
    key = jax.random.fold_in(key, 1)
    k_rows, k_vals = jax.random.split(key, 2)
    columns = 0.4 + 1.6 * jnp.arange(D, dtype=jnp.float32) / (D - 1)
    scales = jnp.exp(jax.random.uniform(k_rows, (TOKENS, 1), jnp.float32, math.log(0.3), math.log(3.0)))
    values = jnp.clip(jax.random.normal(k_vals, (TOKENS, D), jnp.float32), -5.0, 5.0)
    return (values * scales * columns[None, :]).astype(jnp.bfloat16)


def draw_attn(key, part):
    common = common_normal(key)
    return common.astype(jnp.bfloat16)


def draw_attn_tangent(key, part):
    common = common_normal(key)
    key = jax.random.fold_in(key, 3)
    others = jnp.clip(jax.random.normal(key, (TOKENS, D), jnp.float32), -5.0, 5.0)
    return (0.7 * common + 0.7 * others).astype(jnp.bfloat16)


def draw_probe(key, part):
    key = jax.random.fold_in(key, 4)
    return (2 * jax.random.randint(key, (TOKENS, D), 0, 2) - 1).astype(jnp.int32)


def steps_of(stream_key, dims, shards, smallest, high):
    level = 1.0
    for axis_at, blocks in shards:
        draws = jax.random.uniform(jax.random.fold_in(jax.random.fold_in(stream_key, 6), axis_at), (blocks,), jnp.float32, smallest / len(shards), high / len(shards))
        level = level * jnp.repeat(jnp.exp(draws), dims[axis_at] // blocks).reshape((-1,) + (1,) * (len(dims) - 1 - axis_at))
    return level


def centred(key, shape, spread, reach, pieces=(), held_as=jnp.bfloat16):
    values = spread * jax.random.normal(key, shape, jnp.float32)
    if pieces:
        values = values * steps_of(key, shape, pieces, -0.22, 0.18)
    return jnp.clip(values, -reach, reach).astype(held_as)


def setup_inputs(seed: int = 0) -> dict:
    splits = jax.random.split(jax.random.key(seed), 8)
    return {
        "resid": draw_resid(jax.random.fold_in(splits[7], 71), 0),
        "attn": draw_attn(jax.random.fold_in(splits[7], 71), 0),
        "attn_tangent": draw_attn_tangent(jax.random.fold_in(splits[7], 71), 0),
        "probe": draw_probe(jax.random.fold_in(splits[7], 71), 0),
        "norm_gain": jnp.clip(1.0 + 0.18 * jax.random.normal(splits[4], (D,), jnp.float32), 0.1, 1.9),
        "gate_weight": centred(splits[5], (D, FF), D ** -0.5, 0.078125, ((0, 16), (1, 8))),
        "up_weight": centred(splits[6], (D, FF), D ** -0.5, 0.078125, ((0, 16), (1, 8))),
    }


EPS = 1e-06

def reference(resid, attn, attn_tangent, probe, norm_gain, gate_weight, up_weight):
    state = (resid.astype(jnp.float32) + attn.astype(jnp.float32)).astype(jnp.bfloat16)
    state_tangent = (probe.astype(jnp.float32) + attn_tangent.astype(jnp.float32)).astype(jnp.bfloat16)
    yval = state.astype(jnp.float32)
    tval = state_tangent.astype(jnp.float32)
    msq = lax.optimization_barrier(jnp.mean(yval * yval, axis=1, keepdims=True))
    cross = lax.optimization_barrier(jnp.mean(yval * tval, axis=1, keepdims=True))
    rate = lax.rsqrt(msq + EPS)
    normed = (yval * rate * norm_gain).astype(jnp.bfloat16)
    normed_tan = (norm_gain * rate * (tval - yval * (cross * rate * rate))).astype(jnp.bfloat16)
    gate = jnp.dot(normed, gate_weight, preferred_element_type=jnp.float32)
    upper = jnp.dot(normed, up_weight, preferred_element_type=jnp.float32)
    gate_t = jnp.dot(normed_tan, gate_weight, preferred_element_type=jnp.float32)
    upper_t = jnp.dot(normed_tan, up_weight, preferred_element_type=jnp.float32)
    sig = jax.nn.sigmoid(gate)
    active = gate * sig
    hidden = (active * upper).astype(jnp.bfloat16)
    slope = sig * (1.0 + gate * (1.0 - sig))
    hidden_tangent = (slope * gate_t * upper + active * upper_t).astype(jnp.bfloat16)
    return (state, state_tangent, hidden, hidden_tangent)
```

```python
import functools

import jax
import jax.numpy as jnp
from jax import lax
from jax.experimental import pallas as pl
from jax.experimental.pallas import tpu as pltpu
from jax.sharding import PartitionSpec as P

MESH = pl.DeviceIdType.MESH
EPS = 1e-06
D = 6144
TOK = 512
HALF = TOK // 2
FEAT = 768
DEPTH = 384
HID = 1024
UNIT = 128
CHUNKS = HID // UNIT
MM_TOK = 256
NORM_TOK = 16

FROM_PREV, FROM_NEXT, OPP_LO, OPP_HI = 0, 1, 2, 3
LINE_PREV, LINE_NEXT, LINE_LO, LINE_HI = 4, 8, 12, 16


def body(
    resid, attn, attn_tan, probe, gain, gate_w, up_w,
    state_out, state_tan_out, hid_out, hid_tan_out,
    weights, acts, raw, spare, gains, in_res, in_att, in_tan, in_pro,
    w_send, w_recv, a_send, a_recv, loc,
):
    row, col = lax.axis_index("row"), lax.axis_index("col")
    z, x, y, core = row // 4, row % 4, col // 2, col % 2

    def near(pos, axis, step):
        if axis == "z":
            return {"row": ((z + step) % 4) * 4 + x, "col": col}
        if axis == "x":
            return {"row": z * 4 + (x + step) % 4, "col": col}
        return {"row": row, "col": ((y + step) % 4) * 2 + core}

    to = {(a, s): near(None, a, s) for a in "xyz" for s in (1, -1)}
    sibling = {"row": row, "col": y * 2 + 1 - core}

    loads = [
        pltpu.make_async_copy(src, dst, loc.at[n])
        for n, (src, dst) in enumerate(
            ((resid, in_res), (attn, in_att), (attn_tan, in_tan), (probe, in_pro))
        )
    ]

    def stage(j, n):
        cols = pl.ds(pl.multiple_of(j * UNIT, UNIT), UNIT)
        mine = weights.at[j, z, x]
        return (
            pltpu.make_async_copy(gate_w.at[:, cols], mine.at[:, pl.ds(0, UNIT)], loc.at[4 + 2 * n]),
            pltpu.make_async_copy(up_w.at[:, cols], mine.at[:, pl.ds(UNIT, UNIT)], loc.at[5 + 2 * n]),
        )

    staged = [stage(j, j) for j in range(CHUNKS)]
    for pair in staged:
        for copy in pair:
            copy.start()
    for copy in loads:
        copy.start()

    barrier = pltpu.get_barrier_semaphore()
    for other in (*to.values(), sibling):
        pl.semaphore_signal(barrier, inc=1, device_id=other, device_id_type=MESH)
    pl.semaphore_wait(barrier, 7)

    def axes(kind):
        return ("x", "z") if kind == 0 else ("z", "x")

    def spot(kind, j, first, second):
        if kind == 0:
            return weights.at[j, (z + second) % 4, (x + first) % 4]
        return weights.at[j, (z + first) % 4, (x + second) % 4]

    def wsend(j, ref, sem, msg, axis, step):
        return pltpu.make_async_remote_copy(
            src_ref=ref, dst_ref=ref, send_sem=w_send.at[j, sem], recv_sem=w_recv.at[j, msg],
            device_id=to[axis, step], device_id_type=MESH,
        )

    def wwait(j, ref, msg):
        pltpu.make_async_copy(ref, ref, w_recv.at[j, msg]).wait()

    lo, hi = pl.ds(0, DEPTH // 2), pl.ds(DEPTH // 2, DEPTH // 2)

    def own(kind, j):
        a, b = axes(kind)
        mine = spot(kind, j, 0, 0)
        wsend(j, mine, 0, FROM_PREV, a, 1).start()
        wsend(j, mine, 1, FROM_NEXT, a, -1).start()
        wsend(j, mine, 2, LINE_PREV, b, 1).start()
        wsend(j, mine, 3, LINE_NEXT, b, -1).start()

    def first_near(kind, j):
        a, b = axes(kind)
        prev, nxt = spot(kind, j, -1, 0), spot(kind, j, 1, 0)
        wwait(j, prev, FROM_PREV)
        wsend(j, prev.at[lo], 4, OPP_LO, a, 1).start()
        wsend(j, prev, 5, LINE_PREV + 1, b, 1).start()
        wsend(j, prev, 6, LINE_NEXT + 1, b, -1).start()
        wwait(j, nxt, FROM_NEXT)
        wsend(j, nxt.at[hi], 7, OPP_HI, a, -1).start()
        wsend(j, nxt, 8, LINE_PREV + 2, b, 1).start()
        wsend(j, nxt, 9, LINE_NEXT + 2, b, -1).start()

    def first_far(kind, j):
        _, b = axes(kind)
        opp = spot(kind, j, 2, 0)
        wwait(j, opp.at[lo], OPP_LO)
        wwait(j, opp.at[hi], OPP_HI)
        wsend(j, opp, 10, LINE_PREV + 3, b, 1).start()
        wsend(j, opp, 11, LINE_NEXT + 3, b, -1).start()

    firsts = (0, -1, 1, 2)

    def second_near(kind, j):
        _, b = axes(kind)
        for q, first in enumerate(firsts):
            prev, nxt = spot(kind, j, first, -1), spot(kind, j, first, 1)
            wwait(j, prev, LINE_PREV + q)
            wsend(j, prev.at[lo], 12 + q, LINE_LO + q, b, 1).start()
            wwait(j, nxt, LINE_NEXT + q)
            wsend(j, nxt.at[hi], 16 + q, LINE_HI + q, b, -1).start()

    def second_far(kind, j):
        for q, first in enumerate(firsts):
            opp = spot(kind, j, first, 2)
            wwait(j, opp.at[lo], LINE_LO + q)
            wwait(j, opp.at[hi], LINE_HI + q)

    def drain(kind, j):
        _, b = axes(kind)
        whole, half = spot(kind, j, 0, 0), spot(kind, j, 0, 0).at[lo]
        for sem in range(20):
            ref = half if sem in (4, 7) or sem >= 12 else whole
            pltpu.make_async_copy(ref, ref, w_send.at[j, sem]).wait()

    for j in range(CHUNKS):
        for copy in staged[j]:
            copy.wait()
        if j < 3:
            own(j % 2, j)

    for copy in loads:
        copy.wait()
    gains[y, core] = jnp.broadcast_to(gain[...], (8, FEAT))

    def add(rows, target):
        def step(n, _):
            here = pl.ds(pl.multiple_of(rows + n * 32, 32), 32)
            there = pl.ds(pl.multiple_of(n * 32, 32), 32)
            target[0, there, :] = (
                in_res[here, :].astype(jnp.float32) + in_att[here, :].astype(jnp.float32)
            ).astype(jnp.bfloat16)
            target[1, there, :] = (
                in_pro[here, :].astype(jnp.float32) + in_tan[here, :].astype(jnp.float32)
            ).astype(jnp.bfloat16)
            return 0

        lax.fori_loop(0, HALF // 32, step, 0)

    def asend(ref, dst, sem, msg, device):
        return pltpu.make_async_remote_copy(
            src_ref=ref, dst_ref=dst, send_sem=a_send.at[sem], recv_sem=a_recv.at[msg],
            device_id=device, device_id_type=MESH,
        )

    def await_(ref, sem):
        pltpu.make_async_copy(ref, ref, sem).wait()

    add((1 - core) * HALF, spare)
    raw_mine, raw_sib = raw.at[y, core], raw.at[y, 1 - core]
    gain_mine, gain_sib = gains.at[y, core], gains.at[y, 1 - core]
    asend(spare, raw_mine, 0, 0, sibling).start()
    asend(gain_mine, gain_mine, 1, 1, sibling).start()
    add(core * HALF, raw_mine)
    asend(raw_mine, raw_mine, 2, 2, to["y", 1]).start()
    asend(raw_mine, raw_mine, 3, 3, to["y", -1]).start()
    stores = []
    for n, (half, src) in enumerate((((1 - core), spare), (core, raw_mine))):
        rows = pl.ds(pl.multiple_of(half * HALF, HALF), HALF)
        stores.append(pltpu.make_async_copy(src.at[0], state_out.at[rows], loc.at[20 + 2 * n]))
        stores.append(pltpu.make_async_copy(src.at[1], state_tan_out.at[rows], loc.at[21 + 2 * n]))
    for copy in stores:
        copy.start()
    await_(raw_sib, a_recv.at[0])
    await_(gain_sib, a_recv.at[1])
    asend(raw_sib, raw_sib, 4, 4, to["y", 1]).start()
    asend(raw_sib, raw_sib, 5, 5, to["y", -1]).start()
    gain_row = gains.at[y]
    asend(gain_row, gain_row, 6, 6, to["y", 1]).start()
    asend(gain_row, gain_row, 7, 7, to["y", -1]).start()

    prev_y, next_y, opp_y = (y + 3) % 4, (y + 1) % 4, (y + 2) % 4

    def acts_near():
        await_(raw.at[prev_y, core], a_recv.at[2])
        asend(raw.at[prev_y, core], raw.at[prev_y, core], 8, 8, to["y", 1]).start()
        await_(raw.at[next_y, core], a_recv.at[3])
        await_(raw.at[prev_y, 1 - core], a_recv.at[4])
        await_(raw.at[next_y, 1 - core], a_recv.at[5])
        asend(raw.at[next_y, 1 - core], raw.at[next_y, 1 - core], 9, 9, to["y", -1]).start()
        await_(gains.at[prev_y], a_recv.at[6])
        await_(gains.at[next_y], a_recv.at[7])
        asend(gains.at[prev_y], gains.at[prev_y], 10, 10, to["y", 1]).start()

    def acts_far():
        await_(raw.at[opp_y, core], a_recv.at[8])
        await_(raw.at[opp_y, 1 - core], a_recv.at[9])
        await_(gains.at[opp_y], a_recv.at[10])

        def step(n, _):
            rows = pl.ds(pl.multiple_of(n * NORM_TOK, NORM_TOK), NORM_TOK)
            squares = jnp.zeros((NORM_TOK, FEAT), jnp.float32)
            crossed = jnp.zeros((NORM_TOK, FEAT), jnp.float32)
            for g in range(4):
                for p in range(2):
                    yval = raw[g, p, 0, rows, :].astype(jnp.float32)
                    tval = raw[g, p, 1, rows, :].astype(jnp.float32)
                    squares += yval * yval
                    crossed += yval * tval
            rate = lax.rsqrt(jnp.sum(squares, axis=1, keepdims=True) / D + EPS)
            cross = jnp.sum(crossed, axis=1, keepdims=True) / D
            pull = cross * rate * rate
            to_rows = pl.ds(pl.multiple_of(core * HALF + n * NORM_TOK, NORM_TOK), NORM_TOK)
            for g in range(4):
                for p in range(2):
                    yval = raw[g, p, 0, rows, :].astype(jnp.float32)
                    tval = raw[g, p, 1, rows, :].astype(jnp.float32)
                    scale = gains[g, p, 0:1, :]
                    cols = pl.ds((2 * g + p) * FEAT, FEAT)
                    acts[0, to_rows, cols] = (yval * rate * scale).astype(jnp.bfloat16)
                    acts[1, to_rows, cols] = (scale * rate * (tval - yval * pull)).astype(jnp.bfloat16)
            return 0

        lax.fori_loop(0, HALF // NORM_TOK, step, 0)
        done = acts.at[:, pl.ds(pl.multiple_of(core * HALF, HALF), HALF), :]
        asend(done, done, 11, 11, sibling).start()

    def acts_whole():
        other = acts.at[:, pl.ds(pl.multiple_of((1 - core) * HALF, HALF), HALF), :]
        await_(other, a_recv.at[11])

    def multiply(j):
        def step(n, _):
            rows = pl.ds(pl.multiple_of(n * MM_TOK, MM_TOK), MM_TOK)
            lhs = jnp.concatenate([acts[0, rows, :], acts[1, rows, :]], axis=0)
            out = jnp.dot(lhs, weights[j].reshape(D, 2 * UNIT), preferred_element_type=jnp.float32)
            gate, upper = out[:MM_TOK, :UNIT], out[:MM_TOK, UNIT:]
            gate_t, upper_t = out[MM_TOK:, :UNIT], out[MM_TOK:, UNIT:]
            sig = jax.nn.sigmoid(gate)
            active = gate * sig
            slope = sig * (1.0 + gate * (1.0 - sig))
            cols = pl.ds(pl.multiple_of(j * UNIT, UNIT), UNIT)
            hid_out[rows, cols] = (active * upper).astype(jnp.bfloat16)
            hid_tan_out[rows, cols] = (slope * gate_t * upper + active * upper_t).astype(jnp.bfloat16)
            return 0

        lax.fori_loop(0, TOK // MM_TOK, step, 0)

    def slot(t, kind):
        pl.when(t + 3 < CHUNKS)(lambda: own(1 - kind, t + 3))
        pl.when(t < CHUNKS)(lambda: first_near(kind, t))
        pl.when((t >= 1) & (t - 1 < CHUNKS))(lambda: second_near(1 - kind, t - 1))
        pl.when(t < CHUNKS)(lambda: first_far(kind, t))
        pl.when((t >= 2) & (t - 2 < CHUNKS))(lambda: second_far(kind, t - 2))
        if kind == 1:
            pl.when(t == 3)(acts_near)
            pl.when(t == 5)(acts_whole)
        else:
            pl.when(t == 4)(acts_far)
        begin = jnp.where(t < 5, 0, jnp.minimum(2 * (t - 5), t - 2))
        end = jnp.where(t < 5, 0, jnp.minimum(2 * (t - 4), t - 1))

        def item(j, _):
            multiply(j)
            return 0

        lax.fori_loop(begin, end, item, 0)

    def pair(n, _):
        slot(2 * n, 0)
        slot(2 * n + 1, 1)
        return 0

    lax.fori_loop(0, (CHUNKS + 2) // 2, pair, 0)

    def finish(n, _):
        drain(0, 2 * n)
        drain(1, 2 * n + 1)
        return 0

    lax.fori_loop(0, CHUNKS // 2, finish, 0)
    done = acts.at[:, pl.ds(pl.multiple_of(core * HALF, HALF), HALF), :]
    for sem, ref in (
        (0, spare), (1, gain_mine), (2, raw_mine), (3, raw_mine), (4, raw_sib), (5, raw_sib),
        (6, gain_row), (7, gain_row), (8, raw_mine), (9, raw_mine), (10, gain_row), (11, done),
    ):
        await_(ref, a_send.at[sem])
    for copy in stores:
        copy.wait()


def local(resid, attn, attn_tangent, probe, norm_gain, gate_weight, up_weight):
    hbm, vmem = pl.BlockSpec(memory_space=pl.ANY), pl.BlockSpec(memory_space=pltpu.VMEM)
    bf16, f32 = jnp.bfloat16, jnp.float32
    return pl.pallas_call(
        body,
        name="block",
        out_shape=(
            jax.ShapeDtypeStruct((TOK, FEAT), bf16),
            jax.ShapeDtypeStruct((TOK, FEAT), bf16),
            jax.ShapeDtypeStruct((TOK, HID), bf16),
            jax.ShapeDtypeStruct((TOK, HID), bf16),
        ),
        in_specs=[hbm, hbm, hbm, hbm, vmem, hbm, hbm],
        out_specs=(hbm, hbm, vmem, vmem),
        scratch_shapes=[
            pltpu.VMEM((CHUNKS, 4, 4, DEPTH, 2 * UNIT), bf16),
            pltpu.VMEM((2, TOK, D), bf16),
            pltpu.VMEM((4, 2, 2, HALF, FEAT), bf16),
            pltpu.VMEM((2, HALF, FEAT), bf16),
            pltpu.VMEM((4, 2, 8, FEAT), f32),
            pltpu.VMEM((TOK, FEAT), bf16),
            pltpu.VMEM((TOK, FEAT), bf16),
            pltpu.VMEM((TOK, FEAT), bf16),
            pltpu.VMEM((TOK, FEAT), jnp.int32),
            pltpu.SemaphoreType.DMA((CHUNKS, 20)),
            pltpu.SemaphoreType.DMA((CHUNKS, 20)),
            pltpu.SemaphoreType.DMA((12,)),
            pltpu.SemaphoreType.DMA((12,)),
            pltpu.SemaphoreType.DMA((24,)),
        ],
        compiler_params=pltpu.CompilerParams(
            collective_id=0, has_side_effects=True, vmem_limit_bytes=60 << 20
        ),
    )(resid, attn, attn_tangent, probe, norm_gain.reshape(1, FEAT), gate_weight, up_weight)


def solution(mesh):
    in_specs = (
        P("row", "col"),
        P("row", "col"),
        P("row", "col"),
        P("row", "col"),
        P("col"),
        P("row", "col"),
        P("row", "col"),
    )
    out_specs = (P("row", "col"), P("row", "col"), P("row", "col"), P("row", "col"))
    return jax.shard_map(local, mesh=mesh, in_specs=in_specs, out_specs=out_specs, check_vma=False)
```

```python
import jax
import jax.numpy as jnp
from jax import lax
from jax.experimental import pallas as pl
from jax.experimental.pallas import tpu as pltpu
from jax.sharding import PartitionSpec as P

MESH = pl.DeviceIdType.MESH
EPS = 1e-06
D = 6144
TOK = 512
HALF = TOK // 2
SUB = 64
FEAT = 768
DEPTH = 384
HID = 1024
UNIT = 128
CHUNKS = HID // 2 // UNIT
EARLY = (CHUNKS - 1) * UNIT
STEPS = 8
RAW = 6


def body(
    resid, attn, attn_tan, probe, gain, gate_w, up_w,
    state_out, state_tan_out, hid_out, hid_tan_out,
    weights, others, acts, raw, spare, gains, results, in_res, in_att, in_tan, in_pro,
    w_send, w_recv, y_send, y_recv, n_send, n_recv, c_send, c_recv, a_send, a_recv, loc,
):
    row, col = lax.axis_index("row"), lax.axis_index("col")
    z, x, y, core = row // 4, row % 4, col // 2, col % 2
    parity = x % 2

    def at_x(step):
        return {"row": z * 4 + (x + step + 4) % 4, "col": col}

    def at_z(step):
        return {"row": ((z + step + 4) % 4) * 4 + x, "col": col}

    def at_y(step):
        return {"row": row, "col": ((y + step + 4) % 4) * 2 + core}

    sibling = {"row": row, "col": y * 2 + 1 - core}
    x_to = at_x(2 * core - 1)

    def send(src, dst, send_sem, recv_sem, device):
        pltpu.make_async_remote_copy(
            src_ref=src, dst_ref=dst, send_sem=send_sem, recv_sem=recv_sem,
            device_id=device, device_id_type=MESH,
        ).start()

    def await_(ref, sem):
        pltpu.make_async_copy(ref, ref, sem).wait()

    def stage(j, n, half, target):
        cols = pl.ds(pl.multiple_of(half * (HID // 2) + j * UNIT, UNIT), UNIT)
        return (
            pltpu.make_async_copy(gate_w.at[:, cols], target.at[:, pl.ds(0, UNIT)], loc.at[4 + 2 * n]),
            pltpu.make_async_copy(up_w.at[:, cols], target.at[:, pl.ds(UNIT, UNIT)], loc.at[5 + 2 * n]),
        )

    staged = [
        (stage(j, 2 * j, parity, weights.at[j, z, x]), stage(j, 2 * j + 1, 1 - parity, others.at[j]))
        for j in range(CHUNKS)
    ]
    for pairs in staged:
        for pair in pairs:
            for copy in pair:
                copy.start()
    loads = [
        pltpu.make_async_copy(src, dst, loc.at[n])
        for n, (src, dst) in enumerate(
            ((resid, in_res), (attn, in_att), (attn_tan, in_tan), (probe, in_pro))
        )
    ]
    for copy in loads:
        copy.start()

    barrier = pltpu.get_barrier_semaphore()
    for other in (at_x(1), at_x(-1), at_x(2), at_y(1), at_y(-1), at_z(1), at_z(-1), sibling):
        pl.semaphore_signal(barrier, inc=1, device_id=other, device_id_type=MESH)
    pl.semaphore_wait(barrier, 8)

    lo, hi = pl.ds(0, DEPTH // 2), pl.ds(DEPTH // 2, DEPTH // 2)
    firsts = (0, -1, 1, 2)

    def spot(j, q, step):
        return weights.at[j, (z + step + 4) % 4, (x + firsts[q] + 4) % 4]

    def send_x(j):
        mine = weights.at[j, z, x]
        send(others.at[j], mine, w_send.at[j, 0], w_recv.at[j, 0], at_x(1))
        send(others.at[j], mine, w_send.at[j, 1], w_recv.at[j, 1], at_x(-1))
        send(mine, mine, w_send.at[j, 2], w_recv.at[j, 2], at_x(2))

    def send_z(j, q):
        block = spot(j, q, 0)
        send(block, block, w_send.at[j, 3 + q], w_recv.at[j, 3 + q], at_z(1))
        send(block, block, w_send.at[j, 7 + q], w_recv.at[j, 7 + q], at_z(-1))

    def along_x(j):
        for q in (1, 2, 3):
            await_(spot(j, q, 0), w_recv.at[j, q - 1])
            send_z(j, q)

    def z_near(j):
        for q in range(4):
            prev, nxt = spot(j, q, -1), spot(j, q, 1)
            await_(prev, w_recv.at[j, 3 + q])
            send(prev.at[lo], prev.at[lo], w_send.at[j, 11 + q], w_recv.at[j, 11 + q], at_z(1))
            await_(nxt, w_recv.at[j, 7 + q])
            send(nxt.at[hi], nxt.at[hi], w_send.at[j, 15 + q], w_recv.at[j, 15 + q], at_z(-1))

    def z_far(j):
        for q in range(4):
            opp = spot(j, q, 2)
            await_(opp.at[lo], w_recv.at[j, 11 + q])
            await_(opp.at[hi], w_recv.at[j, 15 + q])

    for j in range(CHUNKS):
        for pair in staged[j]:
            for copy in pair:
                copy.wait()
        if j < 2:
            send_x(j)
        if j < 3:
            send_z(j, 0)

    for copy in loads:
        copy.wait()
    gains[y, core] = jnp.broadcast_to(gain[...], (8, FEAT))

    def add(half, target):
        def step(s, _):
            for n in range(2):
                here = pl.ds(pl.multiple_of(half * HALF + s * SUB + n * 32, 32), 32)
                there = pl.ds(n * 32, 32)
                target[s, 0, there, :] = (
                    in_res[here, :].astype(jnp.float32) + in_att[here, :].astype(jnp.float32)
                ).astype(jnp.bfloat16)
                target[s, 1, there, :] = (
                    in_pro[here, :].astype(jnp.float32) + in_tan[here, :].astype(jnp.float32)
                ).astype(jnp.bfloat16)
            return 0

        lax.fori_loop(0, HALF // SUB, step, 0)

    own_steps = pl.ds(0, 4)
    raw_mine, raw_sib = raw.at[y, own_steps, core], raw.at[y, own_steps, 1 - core]
    gain_mine, gain_sib, gain_row = gains.at[y, core], gains.at[y, 1 - core], gains.at[y]
    add(1 - core, spare)
    send(spare, raw_mine, a_send.at[0], a_recv.at[0], sibling)
    send(gain_mine, gain_mine, a_send.at[1], a_recv.at[1], sibling)
    add(core, raw_mine)
    stores = []
    for n, (half, src) in enumerate((((1 - core), spare), (core, raw_mine))):
        there = pl.ds(half * 4, 4)
        stores.append(pltpu.make_async_copy(src.at[:, 0], state_out.at[there], loc.at[20 + 2 * n]))
        stores.append(pltpu.make_async_copy(src.at[:, 1], state_tan_out.at[there], loc.at[21 + 2 * n]))
    for copy in stores:
        copy.start()

    def send_y(i):
        block = raw.at[y, i]
        send(block, block, y_send.at[i, 0], y_recv.at[i, 0], at_y(1))
        send(block, block, y_send.at[i, 1], y_recv.at[i, 1], at_y(-1))

    await_(raw_sib, a_recv.at[0])
    send_y(0)
    await_(gain_sib, a_recv.at[1])
    send(gain_row, gain_row, a_send.at[2], a_recv.at[2], at_y(1))
    send(gain_row, gain_row, a_send.at[3], a_recv.at[3], at_y(-1))
    send_y(1)
    along_x(0)
    for s in range(2):
        send(raw.at[y, s], raw.at[y, 4 + s], a_send.at[5 + s], a_recv.at[5 + s], x_to)

    prev_y, next_y, opp_y = (y + 3) % 4, (y + 1) % 4, (y + 2) % 4

    def y_near(i):
        prev, nxt = raw.at[prev_y, i], raw.at[next_y, i]
        await_(prev, y_recv.at[i, 0])
        send(prev.at[0], prev.at[0], y_send.at[i, 2], y_recv.at[i, 2], at_y(1))
        await_(nxt, y_recv.at[i, 1])
        send(nxt.at[1], nxt.at[1], y_send.at[i, 3], y_recv.at[i, 3], at_y(-1))

    def gains_near():
        await_(gains.at[prev_y], a_recv.at[2])
        await_(gains.at[next_y], a_recv.at[3])
        send(gains.at[prev_y], gains.at[prev_y], a_send.at[4], a_recv.at[4], at_y(1))

    def gains_far():
        await_(gains.at[opp_y], a_recv.at[4])

    def y_far(i):
        await_(raw.at[opp_y, i, 0], y_recv.at[i, 2])
        await_(raw.at[opp_y, i, 1], y_recv.at[i, 3])

    def norm(i):
        def step(n, _):
            rows = pl.ds(pl.multiple_of(n * 16, 16), 16)
            squares = jnp.zeros((16, FEAT), jnp.float32)
            crossed = jnp.zeros((16, FEAT), jnp.float32)
            for g in range(4):
                for p in range(2):
                    yval = raw[g, i, p, 0, rows, :].astype(jnp.float32)
                    tval = raw[g, i, p, 1, rows, :].astype(jnp.float32)
                    squares += yval * yval
                    crossed += yval * tval
            rate = lax.rsqrt(jnp.sum(squares, axis=1, keepdims=True) / D + EPS)
            cross = jnp.sum(crossed, axis=1, keepdims=True) / D
            pull = cross * rate * rate
            for g in range(4):
                for p in range(2):
                    yval = raw[g, i, p, 0, rows, :].astype(jnp.float32)
                    tval = raw[g, i, p, 1, rows, :].astype(jnp.float32)
                    scale = gains[g, p, 0:1, :]
                    cols = pl.ds((2 * g + p) * FEAT, FEAT)
                    acts[i, 0, core, rows, cols] = (yval * rate * scale).astype(jnp.bfloat16)
                    acts[i, 1, core, rows, cols] = (scale * rate * (tval - yval * pull)).astype(jnp.bfloat16)
            return 0

        lax.fori_loop(0, SUB // 16, step, 0)

    def send_sibling(i):
        done = acts.at[i, :, core]
        send(done, done, n_send.at[i], n_recv.at[i], sibling)

    def await_sibling(i):
        await_(acts.at[i, :, 1 - core], n_recv.at[i])

    def send_normed(i):
        send(acts.at[i, :, core], acts.at[i + 4, :, core], a_send.at[5 + i], a_recv.at[5 + i], x_to)

    def take_normed(i):
        await_(acts.at[i, :, core], a_recv.at[1 + i])
        send_sibling(i)

    def multiply(j, i):
        out = jnp.dot(
            acts[i].reshape(4 * SUB, D), weights[j].reshape(D, 2 * UNIT), preferred_element_type=jnp.float32
        )
        gate, upper = out[: 2 * SUB, :UNIT], out[: 2 * SUB, UNIT:]
        gate_t, upper_t = out[2 * SUB :, :UNIT], out[2 * SUB :, UNIT:]
        sig = jax.nn.sigmoid(gate)
        active = gate * sig
        slope = sig * (1.0 + gate * (1.0 - sig))
        cols = pl.ds(pl.multiple_of(j * UNIT, UNIT), UNIT)
        rows = pl.ds(pl.multiple_of((i % 4) * SUB, SUB), SUB)
        whose = i // 4
        hidden = (active * upper).astype(jnp.bfloat16)
        hidden_tan = (slope * gate_t * upper + active * upper_t).astype(jnp.bfloat16)
        for c in range(2):
            results[whose, 0, c, rows, cols] = hidden[c * SUB : (c + 1) * SUB]
            results[whose, 1, c, rows, cols] = hidden_tan[c * SUB : (c + 1) * SUB]

    def give(part, do):
        begin, width = (0, EARLY) if part == 0 else (EARLY, UNIT)
        here = pl.ds(begin, width)
        there = pl.ds(pl.multiple_of(parity * (HID // 2) + begin, UNIT), width)
        for k, out in enumerate((hid_out, hid_tan_out)):
            for c in range(2):
                n = 4 * part + 2 * k + c
                do(n, results.at[1, k, c, :, here], out.at[pl.ds(c * HALF, HALF), there], at_x(1 - 2 * c))

    def give_start(part):
        give(part, lambda n, src, dst, device: send(src, dst, c_send.at[n], c_recv.at[n], device))

    def keep(part):
        begin, width = (0, EARLY) if part == 0 else (EARLY, UNIT)
        there = pl.ds(pl.multiple_of(parity * (HID // 2) + begin, UNIT), width)
        return [
            pltpu.make_async_copy(
                results.at[0, k, c, :, pl.ds(begin, width)], out.at[pl.ds(c * HALF, HALF), there],
                loc.at[24 + 4 * part + 2 * k + c],
            )
            for k, out in enumerate((hid_out, hid_tan_out))
            for c in range(2)
        ]

    def keep_start(part):
        for copy in keep(part):
            copy.start()

    def slot(t, _):
        @pl.when(t < RAW)
        def _():
            y_near(t)

        @pl.when(t + 2 < RAW)
        def _():
            @pl.when(t + 2 >= 4)
            def _():
                await_(raw.at[y, t + 2], a_recv.at[t + 3])

            send_y(t + 2)

        pl.when(t == 0)(gains_near)
        pl.when(t == 1)(gains_far)

        @pl.when((t % 2 == 1) & (t < 8))
        def _():
            z_near(t // 2)

        pl.when(t == 0)(lambda: along_x(1))
        pl.when(t == 1)(lambda: send_x(2))
        pl.when(t == 2)(lambda: send_x(3))
        pl.when(t == 2)(lambda: send_z(3, 0))
        pl.when(t == 2)(lambda: along_x(2))
        pl.when(t == 4)(lambda: along_x(3))

        @pl.when((t >= 1) & (t - 1 < RAW))
        def _():
            y_far(t - 1)
            norm(t - 1)
            send_sibling(t - 1)
            pl.when((t == 3) | (t == 4))(lambda: send_normed(t - 1))

        pl.when((t == 6) | (t == 7))(lambda: take_normed(t))

        @pl.when((t % 2 == 0) & (t >= 2))
        def _():
            z_far(t // 2 - 1)

        @pl.when((t >= 1) & (t < 8))
        def _():
            await_sibling(t - 1)

        pl.when(t == 7)(lambda: await_sibling(7))

        newest = jnp.maximum(t - 2, 0) // 2
        many = newest + 1
        fresh = jnp.where(t == 8, 8, jnp.where((t % 2 == 0) & (t >= 2), t - 1, 0))
        rest = jnp.where((t < 2) | (t == 8), 0, jnp.where(t == 7, 2 * many, many))

        def item(n, _):
            late = n - fresh
            j = jnp.where(n < fresh, newest, late % many)
            i = jnp.where(n < fresh, jnp.where(t == 8, (n + 4) % 8, n), t - 1 + late // many)
            multiply(j, i)
            pl.when((t == 8) & (n == 3))(lambda: give_start(1))
            return 0

        lax.fori_loop(0, fresh + rest, item, 0)

        @pl.when(t == 7)
        def _():
            give_start(0)
            keep_start(0)

        return 0

    lax.fori_loop(0, 9, slot, 0)
    keep_start(1)

    def drain_weights(j, _):
        block = weights.at[0, 0, 0]
        for n in range(11):
            await_(block, w_send.at[j, n])
        for n in range(11, 19):
            await_(block.at[lo], w_send.at[j, n])
        return 0

    lax.fori_loop(0, CHUNKS, drain_weights, 0)

    def drain_raw(i, _):
        block = raw.at[0, 0]
        for n in range(4):
            await_(block if n < 2 else block.at[0], y_send.at[i, n])
        return 0

    lax.fori_loop(0, RAW, drain_raw, 0)

    def drain_normed(i, _):
        await_(acts.at[0, :, 0], n_send.at[i])
        return 0

    lax.fori_loop(0, STEPS, drain_normed, 0)
    for n, ref in enumerate(
        (spare, gain_mine, gain_row, gain_row, gain_row, raw.at[0, 0], raw.at[0, 0], acts.at[0, :, 0], acts.at[0, :, 0])
    ):
        await_(ref, a_send.at[n])
    for part in range(2):
        def leave(n, src, dst, device):
            await_(src, c_send.at[n])
            await_(src, c_recv.at[n])

        give(part, leave)
        for copy in keep(part):
            copy.wait()
    for copy in stores:
        copy.wait()


def local(resid, attn, attn_tangent, probe, norm_gain, gate_weight, up_weight):
    hbm, vmem = pl.BlockSpec(memory_space=pl.ANY), pl.BlockSpec(memory_space=pltpu.VMEM)
    bf16, f32 = jnp.bfloat16, jnp.float32
    dma = pltpu.SemaphoreType.DMA
    state, state_tan, hidden, hidden_tan = pl.pallas_call(
        body,
        name="block",
        out_shape=(
            jax.ShapeDtypeStruct((TOK // SUB, SUB, FEAT), bf16),
            jax.ShapeDtypeStruct((TOK // SUB, SUB, FEAT), bf16),
            jax.ShapeDtypeStruct((TOK, HID), bf16),
            jax.ShapeDtypeStruct((TOK, HID), bf16),
        ),
        in_specs=[hbm, hbm, hbm, hbm, vmem, hbm, hbm],
        out_specs=(hbm, hbm, hbm, hbm),
        scratch_shapes=[
            pltpu.VMEM((CHUNKS, 4, 4, DEPTH, 2 * UNIT), bf16),
            pltpu.VMEM((CHUNKS, DEPTH, 2 * UNIT), bf16),
            pltpu.VMEM((STEPS, 2, 2, SUB, D), bf16),
            pltpu.VMEM((4, RAW, 2, 2, SUB, FEAT), bf16),
            pltpu.VMEM((4, 2, SUB, FEAT), bf16),
            pltpu.VMEM((4, 2, 8, FEAT), f32),
            pltpu.VMEM((2, 2, 2, HALF, HID // 2), bf16),
            pltpu.VMEM((TOK, FEAT), bf16),
            pltpu.VMEM((TOK, FEAT), bf16),
            pltpu.VMEM((TOK, FEAT), bf16),
            pltpu.VMEM((TOK, FEAT), jnp.int32),
            dma((CHUNKS, 19)), dma((CHUNKS, 19)),
            dma((RAW, 4)), dma((RAW, 4)),
            dma((STEPS,)), dma((STEPS,)),
            dma((8,)), dma((8,)),
            dma((9,)), dma((9,)),
            dma((32,)),
        ],
        compiler_params=pltpu.CompilerParams(
            collective_id=0, has_side_effects=True, vmem_limit_bytes=62 << 20
        ),
    )(resid, attn, attn_tangent, probe, norm_gain.reshape(1, FEAT), gate_weight, up_weight)
    return state.reshape(TOK, FEAT), state_tan.reshape(TOK, FEAT), hidden, hidden_tan


def solution(mesh):
    in_specs = (
        P("row", "col"),
        P("row", "col"),
        P("row", "col"),
        P("row", "col"),
        P("col"),
        P("row", "col"),
        P("row", "col"),
    )
    out_specs = (P("row", "col"), P("row", "col"), P("row", "col"), P("row", "col"))
    return jax.shard_map(local, mesh=mesh, in_specs=in_specs, out_specs=out_specs, check_vma=False)
```

```python
import jax
import jax.numpy as jnp
from jax import lax
from jax.experimental import pallas as pl
from jax.experimental.pallas import tpu as pltpu
from jax.sharding import PartitionSpec as P

MESH = pl.DeviceIdType.MESH
EPS = 1e-06
D = 6144
TOK = 512
HALF = TOK // 2
SUB = 64
FEAT = 768
DEPTH = 384
HID = 1024
UNIT = 128
CHUNKS = HID // 2 // UNIT
STEPS = 8
RAW = 6


def body(
    resid, attn, attn_tan, probe, gain, gate_w, up_w,
    state_out, state_tan_out, hid_out, hid_tan_out,
    weights, others, acts, totals, raw, spare, gains, results, in_res, in_att, in_tan, in_pro,
    w_send, w_recv, y_send, y_recv, n_send, n_recv, c_send, c_recv, a_send, a_recv, loc,
):
    row, col = lax.axis_index("row"), lax.axis_index("col")
    z, x, y, core = row // 4, row % 4, col // 2, col % 2
    parity = x % 2

    def at_x(step):
        return {"row": z * 4 + (x + step + 4) % 4, "col": col}

    def at_z(step):
        return {"row": ((z + step + 4) % 4) * 4 + x, "col": col}

    def at_y(step):
        return {"row": row, "col": ((y + step + 4) % 4) * 2 + core}

    sibling = {"row": row, "col": y * 2 + 1 - core}
    x_to = at_x(2 * core - 1)

    def send(src, dst, send_sem, recv_sem, device):
        pltpu.make_async_remote_copy(
            src_ref=src, dst_ref=dst, send_sem=send_sem, recv_sem=recv_sem,
            device_id=device, device_id_type=MESH,
        ).start()

    def await_(ref, sem):
        pltpu.make_async_copy(ref, ref, sem).wait()

    def stage(j, n, half, target):
        cols = pl.ds(pl.multiple_of(half * (HID // 2) + j * UNIT, UNIT), UNIT)
        return (
            pltpu.make_async_copy(gate_w.at[:, cols], target.at[:, pl.ds(0, UNIT)], loc.at[4 + 2 * n]),
            pltpu.make_async_copy(up_w.at[:, cols], target.at[:, pl.ds(UNIT, UNIT)], loc.at[5 + 2 * n]),
        )

    staged = [
        (stage(j, 2 * j, parity, weights.at[j, z, x]), stage(j, 2 * j + 1, 1 - parity, others.at[j]))
        for j in range(CHUNKS)
    ]
    for pairs in staged:
        for pair in pairs:
            for copy in pair:
                copy.start()
    loads = [
        pltpu.make_async_copy(src, dst, loc.at[n])
        for n, (src, dst) in enumerate(
            ((resid, in_res), (attn, in_att), (attn_tan, in_tan), (probe, in_pro))
        )
    ]
    for copy in loads:
        copy.start()

    barrier = pltpu.get_barrier_semaphore()
    for other in (at_x(1), at_x(-1), at_x(2), at_y(1), at_y(-1), at_z(1), at_z(-1), sibling):
        pl.semaphore_signal(barrier, inc=1, device_id=other, device_id_type=MESH)
    pl.semaphore_wait(barrier, 8)

    lo, hi = pl.ds(0, DEPTH // 2), pl.ds(DEPTH // 2, DEPTH // 2)
    firsts = (0, -1, 1, 2)
    last = CHUNKS - 1

    def line(j, step):
        return weights.at[j, (z + step + 4) % 4]

    def spot(j, q, step):
        return weights.at[j, (z + step + 4) % 4, (x + firsts[q] + 4) % 4]

    def send_x(j):
        mine = weights.at[j, z, x]
        send(others.at[j], mine, w_send.at[j, 0], w_recv.at[j, 0], at_x(1))
        send(others.at[j], mine, w_send.at[j, 1], w_recv.at[j, 1], at_x(-1))
        send(mine, mine, w_send.at[j, 2], w_recv.at[j, 2], at_x(2))

    def send_z(j, q, block):
        send(block, block, w_send.at[j, 3 + q], w_recv.at[j, 3 + q], at_z(1))
        send(block, block, w_send.at[j, 7 + q], w_recv.at[j, 7 + q], at_z(-1))

    def along_x(j):
        for q in (1, 2, 3):
            block = spot(j, q, 0)
            await_(block, w_recv.at[j, q - 1])
            pl.when(j < last)(lambda: send_z(j, q, block))
        pl.when(j == last)(lambda: send_z(j, 0, line(j, 0)))

    def z_near(j):
        for step, sem, half, way in ((-1, 3, lo, 1), (1, 7, hi, -1)):
            @pl.when(j < last)
            def _():
                for q in range(4):
                    await_(spot(j, q, step), w_recv.at[j, sem + q])

            pl.when(j == last)(lambda: await_(line(j, step), w_recv.at[j, sem]))
            part = line(j, step).at[:, half]
            n = 11 if way == 1 else 12
            send(part, part, w_send.at[j, n], w_recv.at[j, n], at_z(way))

    def z_far(j):
        opp = line(j, 2)
        await_(opp.at[:, lo], w_recv.at[j, 11])
        await_(opp.at[:, hi], w_recv.at[j, 12])

    for j in range(CHUNKS):
        for pair in staged[j]:
            for copy in pair:
                copy.wait()
        if j < 2:
            send_x(j)
        if j < 3:
            send_z(j, 0, spot(j, 0, 0))

    for copy in loads:
        copy.wait()
    gains[y, core] = jnp.broadcast_to(gain[...], (8, FEAT))

    def add(half, target):
        def step(s, _):
            for n in range(2):
                here = pl.ds(pl.multiple_of(half * HALF + s * SUB + n * 32, 32), 32)
                there = pl.ds(n * 32, 32)
                target[s, 0, there, :] = (
                    in_res[here, :].astype(jnp.float32) + in_att[here, :].astype(jnp.float32)
                ).astype(jnp.bfloat16)
                target[s, 1, there, :] = (
                    in_pro[here, :].astype(jnp.float32) + in_tan[here, :].astype(jnp.float32)
                ).astype(jnp.bfloat16)
            return 0

        lax.fori_loop(0, HALF // SUB, step, 0)

    own_steps = pl.ds(0, 4)
    raw_mine, raw_sib = raw.at[y, own_steps, core], raw.at[y, own_steps, 1 - core]
    gain_mine, gain_sib, gain_row = gains.at[y, core], gains.at[y, 1 - core], gains.at[y]
    add(1 - core, spare)
    send(spare, raw_mine, a_send.at[0], a_recv.at[0], sibling)
    send(gain_mine, gain_mine, a_send.at[1], a_recv.at[1], sibling)
    add(core, raw_mine)
    stores = []
    for n, (half, src) in enumerate((((1 - core), spare), (core, raw_mine))):
        there = pl.ds(half * 4, 4)
        stores.append(pltpu.make_async_copy(src.at[:, 0], state_out.at[there], loc.at[20 + 2 * n]))
        stores.append(pltpu.make_async_copy(src.at[:, 1], state_tan_out.at[there], loc.at[21 + 2 * n]))
    for copy in stores:
        copy.start()

    def send_y(i):
        block = raw.at[y, i]
        send(block, block, y_send.at[i, 0], y_recv.at[i, 0], at_y(1))
        send(block, block, y_send.at[i, 1], y_recv.at[i, 1], at_y(-1))

    await_(raw_sib, a_recv.at[0])
    send_y(0)
    await_(gain_sib, a_recv.at[1])
    send(gain_row, gain_row, a_send.at[2], a_recv.at[2], at_y(1))
    send(gain_row, gain_row, a_send.at[3], a_recv.at[3], at_y(-1))
    send_y(1)

    def send_raw():
        for s in (2, 3):
            send(raw.at[y, s], raw.at[y, 2 + s], a_send.at[3 + s], a_recv.at[3 + s], x_to)

    prev_y, next_y, opp_y = (y + 3) % 4, (y + 1) % 4, (y + 2) % 4

    def y_near(i):
        prev, nxt = raw.at[prev_y, i], raw.at[next_y, i]
        await_(prev, y_recv.at[i, 0])
        send(prev.at[0], prev.at[0], y_send.at[i, 2], y_recv.at[i, 2], at_y(1))
        await_(nxt, y_recv.at[i, 1])
        send(nxt.at[1], nxt.at[1], y_send.at[i, 3], y_recv.at[i, 3], at_y(-1))

    def gains_near():
        await_(gains.at[prev_y], a_recv.at[2])
        await_(gains.at[next_y], a_recv.at[3])
        send(gains.at[prev_y], gains.at[prev_y], a_send.at[4], a_recv.at[4], at_y(1))

    def gains_far():
        await_(gains.at[opp_y], a_recv.at[4])

    def y_far(i):
        await_(raw.at[opp_y, i, 0], y_recv.at[i, 2])
        await_(raw.at[opp_y, i, 1], y_recv.at[i, 3])

    def norm(i):
        def step(n, _):
            rows = pl.ds(pl.multiple_of(n * 16, 16), 16)
            squares = jnp.zeros((16, FEAT), jnp.float32)
            crossed = jnp.zeros((16, FEAT), jnp.float32)
            for g in range(4):
                for p in range(2):
                    yval = raw[g, i, p, 0, rows, :].astype(jnp.float32)
                    tval = raw[g, i, p, 1, rows, :].astype(jnp.float32)
                    squares += yval * yval
                    crossed += yval * tval
            rate = lax.rsqrt(jnp.sum(squares, axis=1, keepdims=True) / D + EPS)
            cross = jnp.sum(crossed, axis=1, keepdims=True) / D
            pull = cross * rate * rate
            for g in range(4):
                for p in range(2):
                    yval = raw[g, i, p, 0, rows, :].astype(jnp.float32)
                    tval = raw[g, i, p, 1, rows, :].astype(jnp.float32)
                    scale = gains[g, p, 0:1, :]
                    cols = pl.ds((2 * g + p) * FEAT, FEAT)
                    acts[i, 0, core, rows, cols] = (yval * rate * scale).astype(jnp.bfloat16)
                    acts[i, 1, core, rows, cols] = (scale * rate * (tval - yval * pull)).astype(jnp.bfloat16)
            return 0

        lax.fori_loop(0, SUB // 16, step, 0)

    def send_sibling(i):
        done = acts.at[i, :, core]
        send(done, done, n_send.at[i], n_recv.at[i], sibling)

    def await_sibling(i):
        await_(acts.at[i, :, 1 - core], n_recv.at[i])

    def send_normed(i):
        send(acts.at[i, :, core], acts.at[i + 6, :, core], a_send.at[7 + i], a_recv.at[7 + i], x_to)

    def take_normed(i):
        await_(acts.at[i, :, core], a_recv.at[1 + i])
        send_sibling(i)

    ROWS = 4 * SUB

    def finish(j, p, out):
        cols = pl.ds(pl.multiple_of(j * UNIT, UNIT), UNIT)
        for s in range(2):
            vals, tans = out[s * ROWS : s * ROWS + ROWS // 2], out[s * ROWS + ROWS // 2 : (s + 1) * ROWS]
            gate, upper = vals[:, :UNIT], vals[:, UNIT:]
            gate_t, upper_t = tans[:, :UNIT], tans[:, UNIT:]
            sig = jax.nn.sigmoid(gate)
            active = gate * sig
            slope = sig * (1.0 + gate * (1.0 - sig))
            hidden = (active * upper).astype(jnp.bfloat16)
            hidden_tan = (slope * gate_t * upper + active * upper_t).astype(jnp.bfloat16)
            rows = pl.ds(pl.multiple_of((p + p // 2) % 2 * 2 * SUB + s * SUB, SUB), SUB)
            for c in range(2):
                results[p // 2, 0, c, rows, cols] = hidden[c * SUB : (c + 1) * SUB]
                results[p // 2, 1, c, rows, cols] = hidden_tan[c * SUB : (c + 1) * SUB]

    def multiply(j, p):
        lhs, rhs = acts[pl.ds(2 * p, 2)].reshape(2 * ROWS, D), weights[j].reshape(D, 2 * UNIT)
        finish(j, p, jnp.dot(lhs, rhs, preferred_element_type=jnp.float32))

    def part(j, p, step):
        where = (z + step + 4) % 4
        cols = pl.ds(pl.multiple_of(where * (D // 4), D // 4), D // 4)
        lhs = acts[pl.ds(2 * p, 2), :, :, :, cols].reshape(2 * ROWS, D // 4)
        return jnp.dot(lhs, weights[j, where].reshape(D // 4, 2 * UNIT), preferred_element_type=jnp.float32)

    def multiply_near(j, p):
        totals[j % 2, p] = part(j, p, 0) + part(j, p, -1) + part(j, p, 1)

    def multiply_far(j, p):
        finish(j, p, totals[j % 2, p] + part(j, p, 2))

    parts = ((0, 2 * UNIT), (2 * UNIT, UNIT), (3 * UNIT, UNIT))

    def give(part, do):
        begin, width = parts[part]
        here = pl.ds(begin, width)
        there = pl.ds(pl.multiple_of(parity * (HID // 2) + begin, UNIT), width)
        for k, out in enumerate((hid_out, hid_tan_out)):
            for c in range(2):
                n = 4 * part + 2 * k + c
                do(n, results.at[1, k, c, :, here], out.at[pl.ds(c * HALF, HALF), there], at_x(1 - 2 * c))

    def give_start(part):
        give(part, lambda n, src, dst, device: send(src, dst, c_send.at[n], c_recv.at[n], device))

    def keep(part):
        begin, width = parts[part]
        there = pl.ds(pl.multiple_of(parity * (HID // 2) + begin, UNIT), width)
        return [
            pltpu.make_async_copy(
                results.at[0, k, c, :, pl.ds(begin, width)], out.at[pl.ds(c * HALF, HALF), there],
                loc.at[24 + 4 * part + 2 * k + c],
            )
            for k, out in enumerate((hid_out, hid_tan_out))
            for c in range(2)
        ]

    def keep_start(part):
        for copy in keep(part):
            copy.start()

    kinds = ("y_far", "y_near", "along_x", "z_near", "z_far", "take", "sibling")
    whole, near, far = 0, 1, 2
    plan = (
        (dict(along_x=0), ()),
        (dict(y_near=0), ()),
        (dict(along_x=1), ()),
        (dict(y_far=0, y_near=1, z_near=0), ()),
        (dict(along_x=2), ()),
        (dict(y_far=1, y_near=2, z_near=1), ()),
        (dict(along_x=3), ()),
        (dict(z_far=0, sibling=0), ((whole, 0, (0,)),)),
        (dict(y_far=2, y_near=3), ()),
        (dict(z_near=2), ((near, 2, (0,)),)),
        (dict(take=6), ()),
        (dict(y_far=3, y_near=4), ()),
        (dict(z_far=1), ((whole, 1, (0,)),)),
        (dict(sibling=1), ((whole, 0, (1,)), (whole, 1, (1,)))),
        (dict(take=7), ((near, 2, (1,)),)),
        (dict(y_far=4, y_near=5), ()),
        (dict(sibling=3), ((whole, 0, (3,)), (whole, 1, (3,)), (near, 2, (3,)))),
        (dict(y_far=5), ()),
        (dict(z_near=3), ((near, 3, (0, 1, 3)),)),
        (dict(sibling=2), ((whole, 0, (2,)), (whole, 1, (2,)))),
        (dict(), ((near, 2, (2,)), (near, 3, (2,)))),
        (dict(z_far=2), ((far, 2, (2, 3, 0, 1)),)),
        (dict(z_far=3), ((far, 3, (2, 3, 0, 1)),)),
    )
    slots = [sum((e.get(k, -1) + 1) << 4 * n for n, k in enumerate(kinds)) for e, _ in plan]
    items = [[how << 4 | j << 2 | p for how, j, pairs in todo for p in pairs] for _, todo in plan]
    codes = [code for todo in items for code in todo]
    bounds = [sum(len(todo) for todo in items[:u]) for u in range(len(items) + 1)]

    def pick(values, n):
        out = jnp.int32(values[0])
        for at in range(1, len(values)):
            if values[at] != values[at - 1]:
                out = jnp.where(n >= at, jnp.int32(values[at]), out)
        return out

    def slot(u, begin):
        code = pick(slots, u)

        def event(kind):
            def run(act):
                index = (lax.shift_right_logical(code, jnp.int32(4 * kinds.index(kind))) & 15) - 1
                pl.when(index >= 0)(lambda: act(index))

            return run

        @event("y_far")
        def _(i):
            y_far(i)
            pl.when(i == 0)(gains_far)
            norm(i)
            send_sibling(i)
            pl.when(i < 2)(lambda: send_normed(i))

        @event("y_near")
        def _(i):
            y_near(i)
            pl.when(i == 0)(gains_near)

            @pl.when(i + 2 < RAW)
            def _():
                pl.when(i >= 2)(lambda: await_(raw.at[y, i + 2], a_recv.at[i + 3]))
                send_y(i + 2)

        @event("along_x")
        def _(j):
            along_x(j)

            @pl.when(j == 0)
            def _():
                send_x(2)
                send_raw()

            pl.when(j == 1)(lambda: send_x(3))

        event("z_near")(z_near)
        event("z_far")(z_far)
        event("take")(take_normed)

        @event("sibling")
        def _(p):
            await_sibling(2 * p)
            await_sibling(2 * p + 1)

        def item(n, _):
            what = pick(codes, n)
            how, j, p = lax.shift_right_logical(what, jnp.int32(4)), lax.shift_right_logical(what, jnp.int32(2)) & 3, what & 3
            pl.when(how == whole)(lambda: multiply(j, p))
            pl.when(how == near)(lambda: multiply_near(j, p))
            pl.when(how == far)(lambda: multiply_far(j, p))
            pl.when(n == bounds[-3] + 1)(lambda: give_start(1))
            pl.when(n == bounds[-2] + 1)(lambda: give_start(2))
            return 0

        end = pick(bounds[1:], u)
        lax.fori_loop(begin, end, item, 0)

        @pl.when(u == len(plan) - 4)
        def _():
            give_start(0)
            keep_start(0)

        pl.when(u == len(plan) - 2)(lambda: keep_start(1))
        return end

    lax.fori_loop(0, len(plan), slot, jnp.int32(0))
    keep_start(2)

    def drain_weights(j, _):
        block, whole_line = weights.at[0, 0, 0], weights.at[0, 0]
        for n in range(3):
            await_(block, w_send.at[j, n])
        for n in (3, 7):
            pl.when(j == last)(lambda: await_(whole_line, w_send.at[j, n]))

            @pl.when(j < last)
            def _():
                for q in range(4):
                    await_(block, w_send.at[j, n + q])

        for n in (11, 12):
            await_(whole_line.at[:, lo], w_send.at[j, n])
        return 0

    lax.fori_loop(0, CHUNKS, drain_weights, 0)

    def drain_raw(i, _):
        block = raw.at[0, 0]
        for n in range(4):
            await_(block if n < 2 else block.at[0], y_send.at[i, n])
        return 0

    lax.fori_loop(0, RAW, drain_raw, 0)

    def drain_normed(i, _):
        await_(acts.at[0, :, 0], n_send.at[i])
        return 0

    lax.fori_loop(0, STEPS, drain_normed, 0)
    for n, ref in enumerate(
        (spare, gain_mine, gain_row, gain_row, gain_row, raw.at[0, 0], raw.at[0, 0], acts.at[0, :, 0], acts.at[0, :, 0])
    ):
        await_(ref, a_send.at[n])
    for part in range(3):
        def leave(n, src, dst, device):
            await_(src, c_send.at[n])
            await_(src, c_recv.at[n])

        give(part, leave)
        for copy in keep(part):
            copy.wait()
    for copy in stores:
        copy.wait()


def local(resid, attn, attn_tangent, probe, norm_gain, gate_weight, up_weight):
    hbm, vmem = pl.BlockSpec(memory_space=pl.ANY), pl.BlockSpec(memory_space=pltpu.VMEM)
    bf16, f32 = jnp.bfloat16, jnp.float32
    dma = pltpu.SemaphoreType.DMA
    state, state_tan, hidden, hidden_tan = pl.pallas_call(
        body,
        name="block",
        out_shape=(
            jax.ShapeDtypeStruct((TOK // SUB, SUB, FEAT), bf16),
            jax.ShapeDtypeStruct((TOK // SUB, SUB, FEAT), bf16),
            jax.ShapeDtypeStruct((TOK, HID), bf16),
            jax.ShapeDtypeStruct((TOK, HID), bf16),
        ),
        in_specs=[hbm, hbm, hbm, hbm, vmem, hbm, hbm],
        out_specs=(hbm, hbm, hbm, hbm),
        scratch_shapes=[
            pltpu.VMEM((CHUNKS, 4, 4, DEPTH, 2 * UNIT), bf16),
            pltpu.VMEM((CHUNKS, DEPTH, 2 * UNIT), bf16),
            pltpu.VMEM((STEPS, 2, 2, SUB, D), bf16),
            pltpu.VMEM((2, STEPS // 2, 8 * SUB, 2 * UNIT), f32),
            pltpu.VMEM((4, RAW, 2, 2, SUB, FEAT), bf16),
            pltpu.VMEM((4, 2, SUB, FEAT), bf16),
            pltpu.VMEM((4, 2, 8, FEAT), f32),
            pltpu.VMEM((2, 2, 2, HALF, HID // 2), bf16),
            pltpu.VMEM((TOK, FEAT), bf16),
            pltpu.VMEM((TOK, FEAT), bf16),
            pltpu.VMEM((TOK, FEAT), bf16),
            pltpu.VMEM((TOK, FEAT), jnp.int32),
            dma((CHUNKS, 13)), dma((CHUNKS, 13)),
            dma((RAW, 4)), dma((RAW, 4)),
            dma((STEPS,)), dma((STEPS,)),
            dma((12,)), dma((12,)),
            dma((9,)), dma((9,)),
            dma((36,)),
        ],
        compiler_params=pltpu.CompilerParams(
            collective_id=0, has_side_effects=True, vmem_limit_bytes=62 << 20
        ),
    )(resid, attn, attn_tangent, probe, norm_gain.reshape(1, FEAT), gate_weight, up_weight)
    return state.reshape(TOK, FEAT), state_tan.reshape(TOK, FEAT), hidden, hidden_tan


def solution(mesh):
    in_specs = (
        P("row", "col"),
        P("row", "col"),
        P("row", "col"),
        P("row", "col"),
        P("col"),
        P("row", "col"),
        P("row", "col"),
    )
    out_specs = (P("row", "col"), P("row", "col"), P("row", "col"), P("row", "col"))
    return jax.shard_map(local, mesh=mesh, in_specs=in_specs, out_specs=out_specs, check_vma=False)
```

```python
import jax
import jax.numpy as jnp
from jax import lax
from jax.experimental import pallas as pl
from jax.experimental.pallas import tpu as pltpu
from jax.sharding import PartitionSpec as P

MESH = pl.DeviceIdType.MESH
EPS = 1e-06
D = 6144
TOK = 512
HALF = TOK // 2
SUB = 64
FEAT = 768
DEPTH = 384
HID = 1024
UNIT = 128
CHUNKS = HID // 2 // UNIT
STEPS = 8
RAW = 6


def body(
    resid, attn, attn_tan, probe, gain, gate_w, up_w,
    state_out, state_tan_out, hid_out, hid_tan_out,
    weights, others, acts, totals, raw, spare, gains, results, in_res, in_att, in_tan, in_pro,
    w_send, w_recv, y_send, y_recv, n_send, n_recv, c_send, c_recv, a_send, a_recv, loc,
):
    row, col = lax.axis_index("row"), lax.axis_index("col")
    z, x, y, core = row // 4, row % 4, col // 2, col % 2
    parity = x % 2

    def at_x(step):
        return {"row": z * 4 + (x + step + 4) % 4, "col": col}

    def at_z(step):
        return {"row": ((z + step + 4) % 4) * 4 + x, "col": col}

    def at_y(step):
        return {"row": row, "col": ((y + step + 4) % 4) * 2 + core}

    sibling = {"row": row, "col": y * 2 + 1 - core}
    x_to = at_x(2 * core - 1)

    def send(src, dst, send_sem, recv_sem, device):
        pltpu.make_async_remote_copy(
            src_ref=src, dst_ref=dst, send_sem=send_sem, recv_sem=recv_sem,
            device_id=device, device_id_type=MESH,
        ).start()

    def await_(ref, sem):
        pltpu.make_async_copy(ref, ref, sem).wait()

    def stage(j, n, half, target):
        cols = pl.ds(pl.multiple_of(half * (HID // 2) + j * UNIT, UNIT), UNIT)
        return (
            pltpu.make_async_copy(gate_w.at[:, cols], target.at[:, pl.ds(0, UNIT)], loc.at[4 + 2 * n]),
            pltpu.make_async_copy(up_w.at[:, cols], target.at[:, pl.ds(UNIT, UNIT)], loc.at[5 + 2 * n]),
        )

    staged = [
        (stage(j, 2 * j, parity, weights.at[j, z, x]), stage(j, 2 * j + 1, 1 - parity, others.at[j]))
        for j in range(CHUNKS)
    ]
    for pairs in staged:
        for pair in pairs:
            for copy in pair:
                copy.start()
    loads = [
        pltpu.make_async_copy(src, dst, loc.at[n])
        for n, (src, dst) in enumerate(
            ((resid, in_res), (attn, in_att), (attn_tan, in_tan), (probe, in_pro))
        )
    ]
    for copy in loads:
        copy.start()

    barrier = pltpu.get_barrier_semaphore()
    for other in (at_x(1), at_x(-1), at_x(2), at_y(1), at_y(-1), at_z(1), at_z(-1), sibling):
        pl.semaphore_signal(barrier, inc=1, device_id=other, device_id_type=MESH)
    pl.semaphore_wait(barrier, 8)

    lo, hi = pl.ds(0, DEPTH // 2), pl.ds(DEPTH // 2, DEPTH // 2)
    firsts = (0, -1, 1, 2)
    last = CHUNKS - 1

    def line(j, step):
        return weights.at[j, (z + step + 4) % 4]

    def spot(j, q, step):
        return weights.at[j, (z + step + 4) % 4, (x + firsts[q] + 4) % 4]

    def send_x(j):
        mine = weights.at[j, z, x]
        send(others.at[j], mine, w_send.at[j, 0], w_recv.at[j, 0], at_x(1))
        send(others.at[j], mine, w_send.at[j, 1], w_recv.at[j, 1], at_x(-1))
        send(mine, mine, w_send.at[j, 2], w_recv.at[j, 2], at_x(2))

    def send_z(j, q, block):
        send(block, block, w_send.at[j, 3 + q], w_recv.at[j, 3 + q], at_z(1))
        send(block, block, w_send.at[j, 7 + q], w_recv.at[j, 7 + q], at_z(-1))

    def along_x(j):
        for q in (1, 2, 3):
            block = spot(j, q, 0)
            await_(block, w_recv.at[j, q - 1])
            pl.when(j < last)(lambda: send_z(j, q, block))
        pl.when(j == last)(lambda: send_z(j, 0, line(j, 0)))

    def z_near(j):
        for step, sem, half, way in ((-1, 3, lo, 1), (1, 7, hi, -1)):
            @pl.when(j < last)
            def _():
                for q in range(4):
                    await_(spot(j, q, step), w_recv.at[j, sem + q])

            pl.when(j == last)(lambda: await_(line(j, step), w_recv.at[j, sem]))
            part = line(j, step).at[:, half]
            n = 11 if way == 1 else 12
            send(part, part, w_send.at[j, n], w_recv.at[j, n], at_z(way))

    def z_far(j):
        opp = line(j, 2)
        await_(opp.at[:, lo], w_recv.at[j, 11])
        await_(opp.at[:, hi], w_recv.at[j, 12])

    for j in range(CHUNKS):
        for pair in staged[j]:
            for copy in pair:
                copy.wait()
        if j < 2:
            send_x(j)
        if j < 3:
            send_z(j, 0, spot(j, 0, 0))

    for copy in loads:
        copy.wait()
    gains[y, core] = jnp.broadcast_to(gain[...].reshape(1, FEAT), (8, FEAT))

    def add(half, target):
        def step(s, _):
            for n in range(2):
                here = pl.ds(pl.multiple_of(half * HALF + s * SUB + n * 32, 32), 32)
                there = pl.ds(n * 32, 32)
                target[s, 0, there, :] = (
                    in_res[here, :].astype(jnp.float32) + in_att[here, :].astype(jnp.float32)
                ).astype(jnp.bfloat16)
                target[s, 1, there, :] = (
                    in_pro[here, :].astype(jnp.float32) + in_tan[here, :].astype(jnp.float32)
                ).astype(jnp.bfloat16)
            return 0

        lax.fori_loop(0, HALF // SUB, step, 0)

    own_steps = pl.ds(0, 4)
    raw_mine, raw_sib = raw.at[y, own_steps, core], raw.at[y, own_steps, 1 - core]
    gain_mine, gain_sib, gain_row = gains.at[y, core], gains.at[y, 1 - core], gains.at[y]
    add(1 - core, spare)
    send(spare, raw_mine, a_send.at[0], a_recv.at[0], sibling)
    send(gain_mine, gain_mine, a_send.at[1], a_recv.at[1], sibling)
    add(core, raw_mine)
    stores = []
    for n, (half, src) in enumerate((((1 - core), spare), (core, raw_mine))):
        there = pl.ds(half * 4, 4)
        stores.append(pltpu.make_async_copy(src.at[:, 0], state_out.at[there], loc.at[20 + 2 * n]))
        stores.append(pltpu.make_async_copy(src.at[:, 1], state_tan_out.at[there], loc.at[21 + 2 * n]))
    for copy in stores:
        copy.start()

    def send_y(i):
        block = raw.at[y, i]
        send(block, block, y_send.at[i, 0], y_recv.at[i, 0], at_y(1))
        send(block, block, y_send.at[i, 1], y_recv.at[i, 1], at_y(-1))

    await_(raw_sib, a_recv.at[0])
    send_y(0)
    await_(gain_sib, a_recv.at[1])
    send(gain_row, gain_row, a_send.at[2], a_recv.at[2], at_y(1))
    send(gain_row, gain_row, a_send.at[3], a_recv.at[3], at_y(-1))
    send_y(1)

    def send_raw():
        for s in (2, 3):
            send(raw.at[y, s], raw.at[y, 2 + s], a_send.at[3 + s], a_recv.at[3 + s], x_to)

    prev_y, next_y, opp_y = (y + 3) % 4, (y + 1) % 4, (y + 2) % 4

    def y_near(i):
        prev, nxt = raw.at[prev_y, i], raw.at[next_y, i]
        await_(prev, y_recv.at[i, 0])
        send(prev.at[0], prev.at[0], y_send.at[i, 2], y_recv.at[i, 2], at_y(1))
        await_(nxt, y_recv.at[i, 1])
        send(nxt.at[1], nxt.at[1], y_send.at[i, 3], y_recv.at[i, 3], at_y(-1))

    def gains_near():
        await_(gains.at[prev_y], a_recv.at[2])
        await_(gains.at[next_y], a_recv.at[3])
        send(gains.at[prev_y], gains.at[prev_y], a_send.at[4], a_recv.at[4], at_y(1))

    def gains_far():
        await_(gains.at[opp_y], a_recv.at[4])

    def y_far(i):
        await_(raw.at[opp_y, i, 0], y_recv.at[i, 2])
        await_(raw.at[opp_y, i, 1], y_recv.at[i, 3])

    def norm(i):
        def step(n, _):
            rows = pl.ds(pl.multiple_of(n * 16, 16), 16)
            squares = jnp.zeros((16, FEAT), jnp.float32)
            crossed = jnp.zeros((16, FEAT), jnp.float32)
            for g in range(4):
                for p in range(2):
                    yval = raw[g, i, p, 0, rows, :].astype(jnp.float32)
                    tval = raw[g, i, p, 1, rows, :].astype(jnp.float32)
                    squares += yval * yval
                    crossed += yval * tval
            rate = lax.rsqrt(jnp.sum(squares, axis=1, keepdims=True) / D + EPS)
            cross = jnp.sum(crossed, axis=1, keepdims=True) / D
            pull = cross * rate * rate
            for g in range(4):
                for p in range(2):
                    yval = raw[g, i, p, 0, rows, :].astype(jnp.float32)
                    tval = raw[g, i, p, 1, rows, :].astype(jnp.float32)
                    scale = gains[g, p, 0:1, :]
                    cols = pl.ds((2 * g + p) * FEAT, FEAT)
                    acts[i, 0, core, rows, cols] = (yval * rate * scale).astype(jnp.bfloat16)
                    acts[i, 1, core, rows, cols] = (scale * rate * (tval - yval * pull)).astype(jnp.bfloat16)
            return 0

        lax.fori_loop(0, SUB // 16, step, 0)

    def send_sibling(i):
        done = acts.at[i, :, core]
        send(done, done, n_send.at[i], n_recv.at[i], sibling)

    def await_sibling(i):
        await_(acts.at[i, :, 1 - core], n_recv.at[i])

    def send_normed(i):
        send(acts.at[i, :, core], acts.at[i + 6, :, core], a_send.at[7 + i], a_recv.at[7 + i], x_to)

    def take_normed(i):
        await_(acts.at[i, :, core], a_recv.at[1 + i])
        send_sibling(i)

    ROWS = 4 * SUB

    def finish(j, p, out):
        cols = pl.ds(pl.multiple_of(j * UNIT, UNIT), UNIT)
        for s in range(2):
            vals, tans = out[s * ROWS : s * ROWS + ROWS // 2], out[s * ROWS + ROWS // 2 : (s + 1) * ROWS]
            gate, upper = vals[:, :UNIT], vals[:, UNIT:]
            gate_t, upper_t = tans[:, :UNIT], tans[:, UNIT:]
            sig = jax.nn.sigmoid(gate)
            active = gate * sig
            slope = sig * (1.0 + gate * (1.0 - sig))
            hidden = (active * upper).astype(jnp.bfloat16)
            hidden_tan = (slope * gate_t * upper + active * upper_t).astype(jnp.bfloat16)
            rows = pl.ds(pl.multiple_of((p + p // 2) % 2 * 2 * SUB + s * SUB, SUB), SUB)
            for c in range(2):
                results[p // 2, 0, c, rows, cols] = hidden[c * SUB : (c + 1) * SUB]
                results[p // 2, 1, c, rows, cols] = hidden_tan[c * SUB : (c + 1) * SUB]

    def multiply(j, p):
        lhs, rhs = acts[pl.ds(2 * p, 2)].reshape(2 * ROWS, D), weights[j].reshape(D, 2 * UNIT)
        finish(j, p, jnp.dot(lhs, rhs, preferred_element_type=jnp.float32))

    def part(j, p, step):
        where = (z + step + 4) % 4
        cols = pl.ds(pl.multiple_of(where * (D // 4), D // 4), D // 4)
        lhs = acts[pl.ds(2 * p, 2), :, :, :, cols].reshape(2 * ROWS, D // 4)
        return jnp.dot(lhs, weights[j, where].reshape(D // 4, 2 * UNIT), preferred_element_type=jnp.float32)

    def multiply_near(j, p):
        totals[j % 2, p] = part(j, p, 0) + part(j, p, -1) + part(j, p, 1)

    def multiply_far(j, p):
        finish(j, p, totals[j % 2, p] + part(j, p, 2))

    parts = ((0, 2 * UNIT), (2 * UNIT, UNIT), (3 * UNIT, UNIT))

    def give(part, do):
        begin, width = parts[part]
        here = pl.ds(begin, width)
        there = pl.ds(pl.multiple_of(parity * (HID // 2) + begin, UNIT), width)
        for k, out in enumerate((hid_out, hid_tan_out)):
            for c in range(2):
                n = 4 * part + 2 * k + c
                do(n, results.at[1, k, c, :, here], out.at[pl.ds(c * HALF, HALF), there], at_x(1 - 2 * c))

    def give_start(part):
        give(part, lambda n, src, dst, device: send(src, dst, c_send.at[n], c_recv.at[n], device))

    def keep(part):
        begin, width = parts[part]
        there = pl.ds(pl.multiple_of(parity * (HID // 2) + begin, UNIT), width)
        return [
            pltpu.make_async_copy(
                results.at[0, k, c, :, pl.ds(begin, width)], out.at[pl.ds(c * HALF, HALF), there],
                loc.at[24 + 4 * part + 2 * k + c],
            )
            for k, out in enumerate((hid_out, hid_tan_out))
            for c in range(2)
        ]

    def keep_start(part):
        for copy in keep(part):
            copy.start()

    kinds = ("y_far", "y_near", "along_x", "z_near", "z_far", "take", "sibling")
    whole, near, far = 0, 1, 2
    plan = (
        (dict(along_x=0), ()),
        (dict(y_near=0), ()),
        (dict(along_x=1), ()),
        (dict(y_far=0, y_near=1, z_near=0), ()),
        (dict(along_x=2), ()),
        (dict(y_far=1, y_near=2, z_near=1), ()),
        (dict(along_x=3), ()),
        (dict(z_far=0, sibling=0), ((whole, 0, (0,)),)),
        (dict(y_far=2, y_near=3), ()),
        (dict(take=6), ()),
        (dict(z_near=2, y_far=3, y_near=4), ((near, 2, (0,)),)),
        (dict(z_far=1), ((whole, 1, (0,)),)),
        (dict(sibling=1), ((whole, 0, (1,)), (whole, 1, (1,)))),
        (dict(take=7), ((near, 2, (1,)),)),
        (dict(y_far=4, y_near=5), ()),
        (dict(sibling=3), ((whole, 0, (3,)), (whole, 1, (3,)), (near, 2, (3,)))),
        (dict(y_far=5), ()),
        (dict(z_near=3), ((near, 3, (0, 1, 3)),)),
        (dict(sibling=2), ((whole, 0, (2,)), (whole, 1, (2,)))),
        (dict(), ((near, 2, (2,)), (near, 3, (2,)))),
        (dict(z_far=2), ((far, 2, (2, 3)),)),
        (dict(z_far=3), ((far, 3, (2, 3)), (far, 2, (0, 1)), (far, 3, (0, 1)))),
    )
    slots = [sum((e.get(k, -1) + 1) << 4 * n for n, k in enumerate(kinds)) for e, _ in plan]
    items = [[how << 4 | j << 2 | p for how, j, pairs in todo for p in pairs] for _, todo in plan]
    codes = [code for todo in items for code in todo]
    bounds = [sum(len(todo) for todo in items[:u]) for u in range(len(items) + 1)]

    def pick(values, n):
        out = jnp.int32(values[0])
        for at in range(1, len(values)):
            if values[at] != values[at - 1]:
                out = jnp.where(n >= at, jnp.int32(values[at]), out)
        return out

    def slot(u, begin):
        code = pick(slots, u)

        def event(kind):
            def run(act):
                index = (lax.shift_right_logical(code, jnp.int32(4 * kinds.index(kind))) & 15) - 1
                pl.when(index >= 0)(lambda: act(index))

            return run

        @event("y_far")
        def _(i):
            y_far(i)
            pl.when(i == 0)(gains_far)
            norm(i)
            send_sibling(i)
            pl.when(i < 2)(lambda: send_normed(i))

        @event("y_near")
        def _(i):
            y_near(i)
            pl.when(i == 0)(gains_near)

            @pl.when(i + 2 < RAW)
            def _():
                pl.when(i >= 2)(lambda: await_(raw.at[y, i + 2], a_recv.at[i + 3]))
                send_y(i + 2)

        @event("along_x")
        def _(j):
            along_x(j)

            @pl.when(j == 0)
            def _():
                send_x(2)
                send_raw()

            pl.when(j == 1)(lambda: send_x(3))

        event("z_near")(z_near)
        event("z_far")(z_far)
        event("take")(take_normed)

        @event("sibling")
        def _(p):
            await_sibling(2 * p)
            await_sibling(2 * p + 1)

        def item(n, _):
            what = pick(codes, n)
            how, j, p = lax.shift_right_logical(what, jnp.int32(4)), lax.shift_right_logical(what, jnp.int32(2)) & 3, what & 3
            pl.when(how == whole)(lambda: multiply(j, p))
            pl.when(how == near)(lambda: multiply_near(j, p))
            pl.when(how == far)(lambda: multiply_far(j, p))
            pl.when(n == bounds[-3] + 1)(lambda: give_start(1))
            pl.when(n == bounds[-2] + 1)(lambda: give_start(2))
            return 0

        end = pick(bounds[1:], u)
        lax.fori_loop(begin, end, item, 0)

        @pl.when(u == len(plan) - 4)
        def _():
            give_start(0)
            keep_start(0)

        return end

    lax.fori_loop(0, len(plan), slot, jnp.int32(0))
    keep_start(1)
    keep_start(2)

    def drain_weights(j, _):
        block, whole_line = weights.at[0, 0, 0], weights.at[0, 0]
        for n in range(3):
            await_(block, w_send.at[j, n])
        for n in (3, 7):
            pl.when(j == last)(lambda: await_(whole_line, w_send.at[j, n]))

            @pl.when(j < last)
            def _():
                for q in range(4):
                    await_(block, w_send.at[j, n + q])

        for n in (11, 12):
            await_(whole_line.at[:, lo], w_send.at[j, n])
        return 0

    lax.fori_loop(0, CHUNKS, drain_weights, 0)

    def drain_raw(i, _):
        block = raw.at[0, 0]
        for n in range(4):
            await_(block if n < 2 else block.at[0], y_send.at[i, n])
        return 0

    lax.fori_loop(0, RAW, drain_raw, 0)

    def drain_normed(i, _):
        await_(acts.at[0, :, 0], n_send.at[i])
        return 0

    lax.fori_loop(0, STEPS, drain_normed, 0)
    for n, ref in enumerate(
        (spare, gain_mine, gain_row, gain_row, gain_row, raw.at[0, 0], raw.at[0, 0], acts.at[0, :, 0], acts.at[0, :, 0])
    ):
        await_(ref, a_send.at[n])
    for part in range(3):
        def leave(n, src, dst, device):
            await_(src, c_send.at[n])
            await_(src, c_recv.at[n])

        give(part, leave)
        for copy in keep(part):
            copy.wait()
    for copy in stores:
        copy.wait()


def settle(*refs):
    ins, outs, held, sems = refs[:4], refs[4:8], refs[8:12], refs[12]
    pieces = []
    for n in range(4):
        for half in range(2):
            size = ins[n].shape[0] // 2
            rows = pl.ds(half * size, size)
            k = 2 * n + half
            pieces.append((
                pltpu.make_async_copy(ins[n].at[rows], held[n].at[rows], sems.at[0, k]),
                pltpu.make_async_copy(held[n].at[rows], outs[n].at[rows], sems.at[1, k]),
            ))
    for get, _ in pieces:
        get.start()
    for get, put in pieces:
        get.wait()
        put.start()
    for _, put in pieces:
        put.wait()


def local(resid, attn, attn_tangent, probe, norm_gain, gate_weight, up_weight):
    hbm, vmem = pl.BlockSpec(memory_space=pl.ANY), pl.BlockSpec(memory_space=pltpu.VMEM)
    bf16, f32 = jnp.bfloat16, jnp.float32
    dma = pltpu.SemaphoreType.DMA
    found = pl.pallas_call(
        body,
        name="block",
        out_shape=(
            jax.ShapeDtypeStruct((TOK // SUB, SUB, FEAT), bf16),
            jax.ShapeDtypeStruct((TOK // SUB, SUB, FEAT), bf16),
            jax.ShapeDtypeStruct((TOK, HID), bf16),
            jax.ShapeDtypeStruct((TOK, HID), bf16),
        ),
        in_specs=[hbm, hbm, hbm, hbm, vmem, hbm, hbm],
        out_specs=(hbm, hbm, hbm, hbm),
        scratch_shapes=[
            pltpu.VMEM((CHUNKS, 4, 4, DEPTH, 2 * UNIT), bf16),
            pltpu.VMEM((CHUNKS, DEPTH, 2 * UNIT), bf16),
            pltpu.VMEM((STEPS, 2, 2, SUB, D), bf16),
            pltpu.VMEM((2, STEPS // 2, 8 * SUB, 2 * UNIT), f32),
            pltpu.VMEM((4, RAW, 2, 2, SUB, FEAT), bf16),
            pltpu.VMEM((4, 2, SUB, FEAT), bf16),
            pltpu.VMEM((4, 2, 8, FEAT), f32),
            pltpu.VMEM((2, 2, 2, HALF, HID // 2), bf16),
            pltpu.VMEM((TOK, FEAT), bf16),
            pltpu.VMEM((TOK, FEAT), bf16),
            pltpu.VMEM((TOK, FEAT), bf16),
            pltpu.VMEM((TOK, FEAT), jnp.int32),
            dma((CHUNKS, 13)), dma((CHUNKS, 13)),
            dma((RAW, 4)), dma((RAW, 4)),
            dma((STEPS,)), dma((STEPS,)),
            dma((12,)), dma((12,)),
            dma((9,)), dma((9,)),
            dma((36,)),
        ],
        compiler_params=pltpu.CompilerParams(
            collective_id=0, has_side_effects=True, vmem_limit_bytes=62 << 20
        ),
    )(resid, attn, attn_tangent, probe, norm_gain, gate_weight, up_weight)
    state, state_tan, hidden, hidden_tan = pl.pallas_call(
        settle,
        name="settle",
        out_shape=tuple(jax.ShapeDtypeStruct(a.shape, a.dtype) for a in found),
        in_specs=[hbm] * 4,
        out_specs=(hbm,) * 4,
        scratch_shapes=[*(pltpu.VMEM(a.shape, a.dtype) for a in found), dma((2, 8))],
        compiler_params=pltpu.CompilerParams(vmem_limit_bytes=62 << 20),
    )(*found)
    return state.reshape(TOK, FEAT), state_tan.reshape(TOK, FEAT), hidden, hidden_tan


def solution(mesh):
    in_specs = (
        P("row", "col"),
        P("row", "col"),
        P("row", "col"),
        P("row", "col"),
        P("col"),
        P("row", "col"),
        P("row", "col"),
    )
    out_specs = (P("row", "col"), P("row", "col"), P("row", "col"), P("row", "col"))
    return jax.shard_map(local, mesh=mesh, in_specs=in_specs, out_specs=out_specs, check_vma=False)
```

```python
import jax
import jax.numpy as jnp
from jax import lax
from jax.experimental import pallas as pl
from jax.experimental.pallas import tpu as pltpu
from jax.sharding import PartitionSpec as P

MESH = pl.DeviceIdType.MESH
EPS = 1e-06
D = 6144
TOK = 512
HALF = TOK // 2
SUB = 64
FEAT = 768
DEPTH = 384
HID = 1024
UNIT = 128
CHUNKS = HID // 2 // UNIT
STEPS = 8
RAW = 6


def body(
    resid, attn, attn_tan, probe, gain, gate_w, up_w,
    state_out, state_tan_out, hid_out, hid_tan_out,
    weights, others, acts, totals, raw, spare, gains, results, in_res, in_att, in_tan, in_pro,
    w_send, w_recv, y_send, y_recv, n_send, n_recv, c_send, c_recv, a_send, a_recv, loc,
):
    row, col = lax.axis_index("row"), lax.axis_index("col")
    z, x, y, core = row // 4, row % 4, col // 2, col % 2
    parity = x % 2

    def at_x(step):
        return {"row": z * 4 + (x + step + 4) % 4, "col": col}

    def at_z(step):
        return {"row": ((z + step + 4) % 4) * 4 + x, "col": col}

    def at_y(step):
        return {"row": row, "col": ((y + step + 4) % 4) * 2 + core}

    sibling = {"row": row, "col": y * 2 + 1 - core}
    x_to = at_x(2 * core - 1)

    def send(src, dst, send_sem, recv_sem, device):
        pltpu.make_async_remote_copy(
            src_ref=src, dst_ref=dst, send_sem=send_sem, recv_sem=recv_sem,
            device_id=device, device_id_type=MESH,
        ).start()

    def await_(ref, sem):
        pltpu.make_async_copy(ref, ref, sem).wait()

    barrier = pltpu.get_barrier_semaphore()
    for other in (at_x(1), at_x(-1), at_x(2), at_y(1), at_y(-1), at_z(1), at_z(-1), sibling):
        pl.semaphore_signal(barrier, inc=1, device_id=other, device_id_type=MESH)

    def stage(j, n, half, target):
        cols = pl.ds(pl.multiple_of(half * (HID // 2) + j * UNIT, UNIT), UNIT)
        return (
            pltpu.make_async_copy(gate_w.at[:, cols], target.at[:, pl.ds(0, UNIT)], loc.at[4 + 2 * n]),
            pltpu.make_async_copy(up_w.at[:, cols], target.at[:, pl.ds(UNIT, UNIT)], loc.at[5 + 2 * n]),
        )

    staged = [
        (stage(j, 2 * j, parity, weights.at[j, z, x]), stage(j, 2 * j + 1, 1 - parity, others.at[j]))
        for j in range(CHUNKS)
    ]
    for pairs in staged:
        for pair in pairs:
            for copy in pair:
                copy.start()
    loads = [
        pltpu.make_async_copy(src, dst, loc.at[n])
        for n, (src, dst) in enumerate(
            ((resid, in_res), (attn, in_att), (attn_tan, in_tan), (probe, in_pro))
        )
    ]
    for copy in loads:
        copy.start()

    pl.semaphore_wait(barrier, 8)

    lo, hi = pl.ds(0, DEPTH // 2), pl.ds(DEPTH // 2, DEPTH // 2)
    firsts = (0, -1, 1, 2)
    last = CHUNKS - 1

    def line(j, step):
        return weights.at[j, (z + step + 4) % 4]

    def spot(j, q, step):
        return weights.at[j, (z + step + 4) % 4, (x + firsts[q] + 4) % 4]

    def send_x(j):
        mine = weights.at[j, z, x]
        send(others.at[j], mine, w_send.at[j, 0], w_recv.at[j, 0], at_x(1))
        send(others.at[j], mine, w_send.at[j, 1], w_recv.at[j, 1], at_x(-1))
        send(mine, mine, w_send.at[j, 2], w_recv.at[j, 2], at_x(2))

    def send_z(j, q, block):
        send(block, block, w_send.at[j, 3 + q], w_recv.at[j, 3 + q], at_z(1))
        send(block, block, w_send.at[j, 7 + q], w_recv.at[j, 7 + q], at_z(-1))

    def along_x(j):
        for q in (1, 2, 3):
            block = spot(j, q, 0)
            await_(block, w_recv.at[j, q - 1])
            pl.when(j < last)(lambda: send_z(j, q, block))
        pl.when(j == last)(lambda: send_z(j, 0, line(j, 0)))

    def z_near(j):
        for step, sem, half, way in ((-1, 3, lo, 1), (1, 7, hi, -1)):
            @pl.when(j < last)
            def _():
                for q in range(4):
                    await_(spot(j, q, step), w_recv.at[j, sem + q])

            pl.when(j == last)(lambda: await_(line(j, step), w_recv.at[j, sem]))
            part = line(j, step).at[:, half]
            n = 11 if way == 1 else 12
            send(part, part, w_send.at[j, n], w_recv.at[j, n], at_z(way))

    def z_far(j):
        opp = line(j, 2)
        await_(opp.at[:, lo], w_recv.at[j, 11])
        await_(opp.at[:, hi], w_recv.at[j, 12])

    for j in range(CHUNKS):
        for pair in staged[j]:
            for copy in pair:
                copy.wait()
        if j < 3:
            send_z(j, 0, spot(j, 0, 0))
        if j < 2:
            send_x(j)

    for copy in loads:
        copy.wait()
    gains[y, core] = jnp.broadcast_to(gain[...].reshape(1, FEAT), (8, FEAT))

    def add(half, target):
        def step(s, _):
            for n in range(2):
                here = pl.ds(pl.multiple_of(half * HALF + s * SUB + n * 32, 32), 32)
                there = pl.ds(n * 32, 32)
                target[s, 0, there, :] = (
                    in_res[here, :].astype(jnp.float32) + in_att[here, :].astype(jnp.float32)
                ).astype(jnp.bfloat16)
                target[s, 1, there, :] = (
                    in_pro[here, :].astype(jnp.float32) + in_tan[here, :].astype(jnp.float32)
                ).astype(jnp.bfloat16)
            return 0

        lax.fori_loop(0, HALF // SUB, step, 0)

    own_steps = pl.ds(0, 4)
    raw_mine, raw_sib = raw.at[y, own_steps, core], raw.at[y, own_steps, 1 - core]
    gain_mine, gain_sib, gain_row = gains.at[y, core], gains.at[y, 1 - core], gains.at[y]
    add(1 - core, spare)
    send(spare, raw_mine, a_send.at[0], a_recv.at[0], sibling)
    send(gain_mine, gain_mine, a_send.at[1], a_recv.at[1], sibling)
    add(core, raw_mine)
    stores = []
    for n, (half, src) in enumerate((((1 - core), spare), (core, raw_mine))):
        there = pl.ds(half * 4, 4)
        stores.append(pltpu.make_async_copy(src.at[:, 0], state_out.at[there], loc.at[20 + 2 * n]))
        stores.append(pltpu.make_async_copy(src.at[:, 1], state_tan_out.at[there], loc.at[21 + 2 * n]))
    for copy in stores:
        copy.start()

    def send_y(i):
        block = raw.at[y, i]
        send(block, block, y_send.at[i, 0], y_recv.at[i, 0], at_y(1))
        send(block, block, y_send.at[i, 1], y_recv.at[i, 1], at_y(-1))

    await_(raw_sib, a_recv.at[0])
    send_y(0)
    await_(gain_sib, a_recv.at[1])
    send(gain_row, gain_row, a_send.at[2], a_recv.at[2], at_y(1))
    send(gain_row, gain_row, a_send.at[3], a_recv.at[3], at_y(-1))
    send_y(1)

    def send_raw():
        for s in (2, 3):
            send(raw.at[y, s], raw.at[y, 2 + s], a_send.at[3 + s], a_recv.at[3 + s], x_to)

    prev_y, next_y, opp_y = (y + 3) % 4, (y + 1) % 4, (y + 2) % 4

    def y_near(i):
        prev, nxt = raw.at[prev_y, i], raw.at[next_y, i]
        await_(prev, y_recv.at[i, 0])
        send(prev.at[0], prev.at[0], y_send.at[i, 2], y_recv.at[i, 2], at_y(1))
        await_(nxt, y_recv.at[i, 1])
        send(nxt.at[1], nxt.at[1], y_send.at[i, 3], y_recv.at[i, 3], at_y(-1))

    def gains_near():
        await_(gains.at[prev_y], a_recv.at[2])
        await_(gains.at[next_y], a_recv.at[3])
        send(gains.at[prev_y], gains.at[prev_y], a_send.at[4], a_recv.at[4], at_y(1))

    def gains_far():
        await_(gains.at[opp_y], a_recv.at[4])

    def y_far(i):
        await_(raw.at[opp_y, i, 0], y_recv.at[i, 2])
        await_(raw.at[opp_y, i, 1], y_recv.at[i, 3])

    def norm(i):
        def step(n, _):
            rows = pl.ds(pl.multiple_of(n * 16, 16), 16)
            squares = jnp.zeros((16, FEAT), jnp.float32)
            crossed = jnp.zeros((16, FEAT), jnp.float32)
            for g in range(4):
                for p in range(2):
                    yval = raw[g, i, p, 0, rows, :].astype(jnp.float32)
                    tval = raw[g, i, p, 1, rows, :].astype(jnp.float32)
                    squares += yval * yval
                    crossed += yval * tval
            rate = lax.rsqrt(jnp.sum(squares, axis=1, keepdims=True) / D + EPS)
            cross = jnp.sum(crossed, axis=1, keepdims=True) / D
            pull = cross * rate * rate
            for g in range(4):
                for p in range(2):
                    yval = raw[g, i, p, 0, rows, :].astype(jnp.float32)
                    tval = raw[g, i, p, 1, rows, :].astype(jnp.float32)
                    scale = gains[g, p, 0:1, :]
                    cols = pl.ds((2 * g + p) * FEAT, FEAT)
                    acts[i, 0, core, rows, cols] = (yval * rate * scale).astype(jnp.bfloat16)
                    acts[i, 1, core, rows, cols] = (scale * rate * (tval - yval * pull)).astype(jnp.bfloat16)
            return 0

        lax.fori_loop(0, SUB // 16, step, 0)

    def send_sibling(i):
        done = acts.at[i, :, core]
        send(done, done, n_send.at[i], n_recv.at[i], sibling)

    def await_sibling(i):
        await_(acts.at[i, :, 1 - core], n_recv.at[i])

    def send_normed(i):
        send(acts.at[i, :, core], acts.at[i + 6, :, core], a_send.at[7 + i], a_recv.at[7 + i], x_to)

    def take_normed(i):
        await_(acts.at[i, :, core], a_recv.at[1 + i])
        send_sibling(i)

    ROWS = 4 * SUB

    def finish(j, i, out):
        gate, upper = out[: ROWS // 2, :UNIT], out[: ROWS // 2, UNIT:]
        gate_t, upper_t = out[ROWS // 2 :, :UNIT], out[ROWS // 2 :, UNIT:]
        sig = jax.nn.sigmoid(gate)
        active = gate * sig
        slope = sig * (1.0 + gate * (1.0 - sig))
        hidden = (active * upper).astype(jnp.bfloat16)
        hidden_tan = (slope * gate_t * upper + active * upper_t).astype(jnp.bfloat16)
        whose = i // 4
        cols = pl.ds(pl.multiple_of(j * UNIT, UNIT), UNIT)
        rows = pl.ds(pl.multiple_of((i + 2 * whose) % 4 * SUB, SUB), SUB)
        for c in range(2):
            results[whose, 0, c, rows, cols] = hidden[c * SUB : (c + 1) * SUB]
            results[whose, 1, c, rows, cols] = hidden_tan[c * SUB : (c + 1) * SUB]

    def multiply(j, i, count):
        lhs, rhs = acts[pl.ds(i, count)].reshape(count * ROWS, D), weights[j].reshape(D, 2 * UNIT)
        out = jnp.dot(lhs, rhs, preferred_element_type=jnp.float32)
        for s in range(count):
            finish(j, i + s, out[s * ROWS : (s + 1) * ROWS])

    def part(j, i, count, step):
        where = (z + step + 4) % 4
        cols = pl.ds(pl.multiple_of(where * (D // 4), D // 4), D // 4)
        lhs = acts[pl.ds(i, count), :, :, :, cols].reshape(count * ROWS, D // 4)
        return jnp.dot(lhs, weights[j, where].reshape(D // 4, 2 * UNIT), preferred_element_type=jnp.float32)

    def multiply_near(j, i, count):
        out = part(j, i, count, 0) + part(j, i, count, -1) + part(j, i, count, 1)
        totals[j % 2, pl.ds(i, count)] = out.reshape(count, ROWS, 2 * UNIT)

    def multiply_far(j, i, count):
        out = totals[j % 2, pl.ds(i, count)].reshape(count * ROWS, 2 * UNIT) + part(j, i, count, 2)
        for s in range(count):
            finish(j, i + s, out[s * ROWS : (s + 1) * ROWS])

    parts = ((0, 2 * UNIT), (2 * UNIT, UNIT), (3 * UNIT, UNIT))

    def give(part, do):
        begin, width = parts[part]
        here = pl.ds(begin, width)
        there = pl.ds(pl.multiple_of(parity * (HID // 2) + begin, UNIT), width)
        for k, out in enumerate((hid_out, hid_tan_out)):
            for c in range(2):
                n = 4 * part + 2 * k + c
                do(n, results.at[1, k, c, :, here], out.at[pl.ds(c * HALF, HALF), there], at_x(1 - 2 * c))

    def give_start(part):
        give(part, lambda n, src, dst, device: send(src, dst, c_send.at[n], c_recv.at[n], device))

    def keep(part):
        begin, width = parts[part]
        there = pl.ds(pl.multiple_of(parity * (HID // 2) + begin, UNIT), width)
        return [
            pltpu.make_async_copy(
                results.at[0, k, c, :, pl.ds(begin, width)], out.at[pl.ds(c * HALF, HALF), there],
                loc.at[24 + 4 * part + 2 * k + c],
            )
            for k, out in enumerate((hid_out, hid_tan_out))
            for c in range(2)
        ]

    def keep_start(part):
        for copy in keep(part):
            copy.start()

    kinds = ("y_far", "y_near", "along_x", "z_near", "z_far", "take", "sibling")
    whole, near, far, whole_pair, near_pair = 0, 1, 2, 3, 4
    plan = (
        (dict(along_x=0), ()),
        (dict(y_near=0), ()),
        (dict(along_x=1), ()),
        (dict(y_far=0, y_near=1, z_near=0), ()),
        (dict(along_x=2), ()),
        (dict(y_far=1, y_near=2, z_near=1), ()),
        (dict(along_x=3), ()),
        (dict(z_far=0, sibling=0), ()),
        (dict(sibling=1), ((whole_pair, 0, (0,)),)),
        (dict(y_far=2, y_near=3), ()),
        (dict(sibling=2), ((whole, 0, (2,)),)),
        (dict(z_near=2, take=6), ((near_pair, 2, (0,)), (near, 2, (2,)))),
        (dict(sibling=6), ((whole, 0, (6,)), (near, 2, (6,)))),
        (dict(y_far=3, y_near=4), ()),
        (dict(z_far=1), ((whole_pair, 1, (0,)), (whole, 1, (2, 6)))),
        (dict(sibling=3), ((whole, 0, (3,)), (whole, 1, (3,)), (near, 2, (3,)))),
        (dict(take=7), ()),
        (dict(y_far=4, y_near=5), ()),
        (dict(sibling=7), ((whole, 0, (7,)), (whole, 1, (7,)), (near, 2, (7,)))),
        (dict(sibling=4), ((whole, 0, (4,)), (whole, 1, (4,)), (near, 2, (4,)))),
        (dict(y_far=5), ()),
        (dict(z_near=3), ((near_pair, 3, (0, 2, 6)),)),
        (dict(sibling=5), ((whole, 0, (5,)), (whole, 1, (5,)))),
        (dict(), ((near, 2, (5,)), (near_pair, 3, (4,)))),
        (dict(z_far=2), ((far, 2, (4, 6)),)),
        (dict(z_far=3), ((far, 3, (4, 6)), (far, 2, (0, 2)), (far, 3, (0, 2)))),
    )
    slots = [sum((e.get(k, -1) + 1) << 4 * n for n, k in enumerate(kinds)) for e, _ in plan]
    items = [[how << 5 | j << 3 | i for how, j, steps in todo for i in steps] for _, todo in plan]
    codes = [code for todo in items for code in todo]
    bounds = [sum(len(todo) for todo in items[:u]) for u in range(len(items) + 1)]

    def pick(values, n):
        out = jnp.int32(values[0])
        for at in range(1, len(values)):
            if values[at] != values[at - 1]:
                out = jnp.where(n >= at, jnp.int32(values[at]), out)
        return out

    def slot(u, begin):
        code = pick(slots, u)

        def event(kind):
            def run(act):
                index = (lax.shift_right_logical(code, jnp.int32(4 * kinds.index(kind))) & 15) - 1
                pl.when(index >= 0)(lambda: act(index))

            return run

        @event("y_far")
        def _(i):
            y_far(i)
            pl.when(i == 0)(gains_far)
            norm(i)
            send_sibling(i)
            pl.when(i < 2)(lambda: send_normed(i))

        @event("y_near")
        def _(i):
            y_near(i)
            pl.when(i == 0)(gains_near)

            @pl.when(i + 2 < RAW)
            def _():
                pl.when(i >= 2)(lambda: await_(raw.at[y, i + 2], a_recv.at[i + 3]))
                send_y(i + 2)

        @event("along_x")
        def _(j):
            along_x(j)

            @pl.when(j == 0)
            def _():
                send_x(2)
                send_raw()

            pl.when(j == 1)(lambda: send_x(3))

        event("z_near")(z_near)
        event("z_far")(z_far)
        event("take")(take_normed)

        event("sibling")(await_sibling)

        def item(n, _):
            what = pick(codes, n)
            how, j, i = lax.shift_right_logical(what, jnp.int32(5)), lax.shift_right_logical(what, jnp.int32(3)) & 3, what & 7
            pl.when(how == whole)(lambda: multiply(j, i, 1))
            pl.when(how == near)(lambda: multiply_near(j, i, 1))
            pl.when(how == far)(lambda: multiply_far(j, i, 2))
            pl.when(how == whole_pair)(lambda: multiply(j, i, 2))
            pl.when(how == near_pair)(lambda: multiply_near(j, i, 2))
            pl.when(n == bounds[-3] + 1)(lambda: give_start(1))
            pl.when(n == bounds[-2] + 1)(lambda: give_start(2))
            return 0

        end = pick(bounds[1:], u)
        lax.fori_loop(begin, end, item, 0)

        @pl.when(u == len(plan) - 4)
        def _():
            give_start(0)
            keep_start(0)

        return end

    lax.fori_loop(0, len(plan), slot, jnp.int32(0))
    keep_start(1)
    keep_start(2)

    def drain_weights(j, _):
        block, whole_line = weights.at[0, 0, 0], weights.at[0, 0]
        for n in range(3):
            await_(block, w_send.at[j, n])
        for n in (3, 7):
            pl.when(j == last)(lambda: await_(whole_line, w_send.at[j, n]))

            @pl.when(j < last)
            def _():
                for q in range(4):
                    await_(block, w_send.at[j, n + q])

        for n in (11, 12):
            await_(whole_line.at[:, lo], w_send.at[j, n])
        return 0

    lax.fori_loop(0, CHUNKS, drain_weights, 0)

    def drain_raw(i, _):
        block = raw.at[0, 0]
        for n in range(4):
            await_(block if n < 2 else block.at[0], y_send.at[i, n])
        return 0

    lax.fori_loop(0, RAW, drain_raw, 0)

    def drain_normed(i, _):
        await_(acts.at[0, :, 0], n_send.at[i])
        return 0

    lax.fori_loop(0, STEPS, drain_normed, 0)
    for n, ref in enumerate(
        (spare, gain_mine, gain_row, gain_row, gain_row, raw.at[0, 0], raw.at[0, 0], acts.at[0, :, 0], acts.at[0, :, 0])
    ):
        await_(ref, a_send.at[n])
    for part in range(3):
        def leave(n, src, dst, device):
            await_(src, c_send.at[n])
            await_(src, c_recv.at[n])

        give(part, leave)
        for copy in keep(part):
            copy.wait()
    for copy in stores:
        copy.wait()


def settle(*refs):
    ins, outs, held, sems = refs[:4], refs[4:8], refs[8:12], refs[12]
    pieces = []
    for n in range(4):
        for half in range(2):
            size = ins[n].shape[0] // 2
            rows = pl.ds(half * size, size)
            k = 2 * n + half
            pieces.append((
                pltpu.make_async_copy(ins[n].at[rows], held[n].at[rows], sems.at[0, k]),
                pltpu.make_async_copy(held[n].at[rows], outs[n].at[rows], sems.at[1, k]),
            ))
    for get, _ in pieces:
        get.start()
    for get, put in pieces:
        get.wait()
        put.start()
    for _, put in pieces:
        put.wait()


def local(resid, attn, attn_tangent, probe, norm_gain, gate_weight, up_weight):
    hbm, vmem = pl.BlockSpec(memory_space=pl.ANY), pl.BlockSpec(memory_space=pltpu.VMEM)
    bf16, f32 = jnp.bfloat16, jnp.float32
    dma = pltpu.SemaphoreType.DMA
    found = pl.pallas_call(
        body,
        name="block",
        out_shape=(
            jax.ShapeDtypeStruct((TOK // SUB, SUB, FEAT), bf16),
            jax.ShapeDtypeStruct((TOK // SUB, SUB, FEAT), bf16),
            jax.ShapeDtypeStruct((TOK, HID), bf16),
            jax.ShapeDtypeStruct((TOK, HID), bf16),
        ),
        in_specs=[hbm, hbm, hbm, hbm, vmem, hbm, hbm],
        out_specs=(hbm, hbm, hbm, hbm),
        scratch_shapes=[
            pltpu.VMEM((CHUNKS, 4, 4, DEPTH, 2 * UNIT), bf16),
            pltpu.VMEM((CHUNKS, DEPTH, 2 * UNIT), bf16),
            pltpu.VMEM((STEPS, 2, 2, SUB, D), bf16),
            pltpu.VMEM((2, STEPS, 4 * SUB, 2 * UNIT), f32),
            pltpu.VMEM((4, RAW, 2, 2, SUB, FEAT), bf16),
            pltpu.VMEM((4, 2, SUB, FEAT), bf16),
            pltpu.VMEM((4, 2, 8, FEAT), f32),
            pltpu.VMEM((2, 2, 2, HALF, HID // 2), bf16),
            pltpu.VMEM((TOK, FEAT), bf16),
            pltpu.VMEM((TOK, FEAT), bf16),
            pltpu.VMEM((TOK, FEAT), bf16),
            pltpu.VMEM((TOK, FEAT), jnp.int32),
            dma((CHUNKS, 13)), dma((CHUNKS, 13)),
            dma((RAW, 4)), dma((RAW, 4)),
            dma((STEPS,)), dma((STEPS,)),
            dma((12,)), dma((12,)),
            dma((9,)), dma((9,)),
            dma((36,)),
        ],
        compiler_params=pltpu.CompilerParams(
            collective_id=0, has_side_effects=True, vmem_limit_bytes=62 << 20
        ),
    )(resid, attn, attn_tangent, probe, norm_gain, gate_weight, up_weight)
    state, state_tan, hidden, hidden_tan = pl.pallas_call(
        settle,
        name="settle",
        out_shape=tuple(jax.ShapeDtypeStruct(a.shape, a.dtype) for a in found),
        in_specs=[hbm] * 4,
        out_specs=(hbm,) * 4,
        scratch_shapes=[*(pltpu.VMEM(a.shape, a.dtype) for a in found), dma((2, 8))],
        compiler_params=pltpu.CompilerParams(vmem_limit_bytes=62 << 20),
    )(*found)
    return state.reshape(TOK, FEAT), state_tan.reshape(TOK, FEAT), hidden, hidden_tan


def solution(mesh):
    in_specs = (
        P("row", "col"),
        P("row", "col"),
        P("row", "col"),
        P("row", "col"),
        P("col"),
        P("row", "col"),
        P("row", "col"),
    )
    out_specs = (P("row", "col"), P("row", "col"), P("row", "col"), P("row", "col"))
    return jax.shard_map(local, mesh=mesh, in_specs=in_specs, out_specs=out_specs, check_vma=False)
```

```python
import jax
import jax.numpy as jnp
from jax import lax
from jax.experimental import pallas as pl
from jax.experimental.pallas import tpu as pltpu
from jax.sharding import PartitionSpec as P

MESH = pl.DeviceIdType.MESH
EPS = 1e-06
D = 6144
TOK = 512
HALF = TOK // 2
SUB = 64
FEAT = 768
DEPTH = 384
HID = 1024
UNIT = 128
CHUNKS = HID // 2 // UNIT
STEPS = 8
RAW = 6


def body(
    resid, attn, attn_tan, probe, gain, gate_w, up_w,
    state_out, state_tan_out, hid_out, hid_tan_out,
    weights, others, acts, totals, raw, spare, gains, results, in_res, in_att, in_tan, in_pro,
    w_send, w_recv, y_send, y_recv, n_send, n_recv, c_send, c_recv, a_send, a_recv, loc,
):
    row, col = lax.axis_index("row"), lax.axis_index("col")
    z, x, y, core = row // 4, row % 4, col // 2, col % 2
    parity = x % 2

    def at_x(step):
        return {"row": z * 4 + (x + step + 4) % 4, "col": col}

    def at_z(step):
        return {"row": ((z + step + 4) % 4) * 4 + x, "col": col}

    def at_y(step):
        return {"row": row, "col": ((y + step + 4) % 4) * 2 + core}

    sibling = {"row": row, "col": y * 2 + 1 - core}
    x_to = at_x(2 * core - 1)

    def send(src, dst, send_sem, recv_sem, device):
        pltpu.make_async_remote_copy(
            src_ref=src, dst_ref=dst, send_sem=send_sem, recv_sem=recv_sem,
            device_id=device, device_id_type=MESH,
        ).start()

    def await_(ref, sem):
        pltpu.make_async_copy(ref, ref, sem).wait()

    barrier = pltpu.get_barrier_semaphore()
    for other in (at_x(1), at_x(-1), at_x(2), at_y(1), at_y(-1), at_z(1), at_z(-1), sibling):
        pl.semaphore_signal(barrier, inc=1, device_id=other, device_id_type=MESH)

    def stage(j, n, half, target):
        cols = pl.ds(pl.multiple_of(half * (HID // 2) + j * UNIT, UNIT), UNIT)
        return (
            pltpu.make_async_copy(gate_w.at[:, cols], target.at[:, pl.ds(0, UNIT)], loc.at[4 + 2 * n]),
            pltpu.make_async_copy(up_w.at[:, cols], target.at[:, pl.ds(UNIT, UNIT)], loc.at[5 + 2 * n]),
        )

    staged = [
        (stage(j, 2 * j, parity, weights.at[j, z, x]), stage(j, 2 * j + 1, 1 - parity, others.at[j]))
        for j in range(CHUNKS)
    ]
    for pairs in staged:
        for pair in pairs:
            for copy in pair:
                copy.start()
    loads = [
        pltpu.make_async_copy(src, dst, loc.at[n])
        for n, (src, dst) in enumerate(
            ((resid, in_res), (attn, in_att), (attn_tan, in_tan), (probe, in_pro))
        )
    ]
    for copy in loads:
        copy.start()

    pl.semaphore_wait(barrier, 8)

    lo, hi = pl.ds(0, DEPTH // 2), pl.ds(DEPTH // 2, DEPTH // 2)
    firsts = (0, -1, 1, 2)
    last = CHUNKS - 1

    def line(j, step):
        return weights.at[j, (z + step + 4) % 4]

    def spot(j, q, step):
        return weights.at[j, (z + step + 4) % 4, (x + firsts[q] + 4) % 4]

    def send_x(j):
        mine = weights.at[j, z, x]
        send(others.at[j], mine, w_send.at[j, 0], w_recv.at[j, 0], at_x(1))
        send(others.at[j], mine, w_send.at[j, 1], w_recv.at[j, 1], at_x(-1))
        send(mine, mine, w_send.at[j, 2], w_recv.at[j, 2], at_x(2))

    def send_z(j, q, block):
        send(block, block, w_send.at[j, 3 + q], w_recv.at[j, 3 + q], at_z(1))
        send(block, block, w_send.at[j, 7 + q], w_recv.at[j, 7 + q], at_z(-1))

    def along_x(j):
        for q in (1, 2, 3):
            block = spot(j, q, 0)
            await_(block, w_recv.at[j, q - 1])
            pl.when(j < last)(lambda: send_z(j, q, block))
        pl.when(j == last)(lambda: send_z(j, 0, line(j, 0)))

    def z_near(j):
        for step, sem, half, way in ((-1, 3, lo, 1), (1, 7, hi, -1)):
            @pl.when(j < last)
            def _():
                for q in range(4):
                    await_(spot(j, q, step), w_recv.at[j, sem + q])

            pl.when(j == last)(lambda: await_(line(j, step), w_recv.at[j, sem]))
            part = line(j, step).at[:, half]
            n = 11 if way == 1 else 12
            send(part, part, w_send.at[j, n], w_recv.at[j, n], at_z(way))

    def z_far(j):
        opp = line(j, 2)
        await_(opp.at[:, lo], w_recv.at[j, 11])
        await_(opp.at[:, hi], w_recv.at[j, 12])

    for j in range(CHUNKS):
        for pair in staged[j]:
            for copy in pair:
                copy.wait()
        if j < 3:
            send_z(j, 0, spot(j, 0, 0))
        if j < 2:
            send_x(j)

    for copy in loads:
        copy.wait()
    gains[y, core] = jnp.broadcast_to(gain[...].reshape(1, FEAT), (8, FEAT))

    def add(half, target):
        def step(s, _):
            for n in range(2):
                here = pl.ds(pl.multiple_of(half * HALF + s * SUB + n * 32, 32), 32)
                there = pl.ds(n * 32, 32)
                target[s, 0, there, :] = (
                    in_res[here, :].astype(jnp.float32) + in_att[here, :].astype(jnp.float32)
                ).astype(jnp.bfloat16)
                target[s, 1, there, :] = (
                    in_pro[here, :].astype(jnp.float32) + in_tan[here, :].astype(jnp.float32)
                ).astype(jnp.bfloat16)
            return 0

        lax.fori_loop(0, HALF // SUB, step, 0)

    own_steps = pl.ds(0, 4)
    raw_mine, raw_sib = raw.at[y, own_steps, core], raw.at[y, own_steps, 1 - core]
    gain_mine, gain_sib, gain_row = gains.at[y, core], gains.at[y, 1 - core], gains.at[y]
    add(1 - core, spare)
    send(spare, raw_mine, a_send.at[0], a_recv.at[0], sibling)
    send(gain_mine, gain_mine, a_send.at[1], a_recv.at[1], sibling)
    add(core, raw_mine)
    stores = []
    for n, (half, src) in enumerate((((1 - core), spare), (core, raw_mine))):
        there = pl.ds(half * 4, 4)
        stores.append(pltpu.make_async_copy(src.at[:, 0], state_out.at[there], loc.at[20 + 2 * n]))
        stores.append(pltpu.make_async_copy(src.at[:, 1], state_tan_out.at[there], loc.at[21 + 2 * n]))
    for copy in stores:
        copy.start()

    def send_y(i):
        block = raw.at[y, i]
        send(block, block, y_send.at[i, 0], y_recv.at[i, 0], at_y(1))
        send(block, block, y_send.at[i, 1], y_recv.at[i, 1], at_y(-1))

    await_(raw_sib, a_recv.at[0])
    send_y(0)
    await_(gain_sib, a_recv.at[1])
    send(gain_row, gain_row, a_send.at[2], a_recv.at[2], at_y(1))
    send(gain_row, gain_row, a_send.at[3], a_recv.at[3], at_y(-1))
    send_y(1)

    def send_raw():
        for s in (2, 3):
            send(raw.at[y, s], raw.at[y, 2 + s], a_send.at[3 + s], a_recv.at[3 + s], x_to)

    prev_y, next_y, opp_y = (y + 3) % 4, (y + 1) % 4, (y + 2) % 4

    def y_near(i):
        prev, nxt = raw.at[prev_y, i], raw.at[next_y, i]
        await_(prev, y_recv.at[i, 0])
        send(prev.at[0], prev.at[0], y_send.at[i, 2], y_recv.at[i, 2], at_y(1))
        await_(nxt, y_recv.at[i, 1])
        send(nxt.at[1], nxt.at[1], y_send.at[i, 3], y_recv.at[i, 3], at_y(-1))

    def gains_near():
        await_(gains.at[prev_y], a_recv.at[2])
        await_(gains.at[next_y], a_recv.at[3])
        send(gains.at[prev_y], gains.at[prev_y], a_send.at[4], a_recv.at[4], at_y(1))

    def gains_far():
        await_(gains.at[opp_y], a_recv.at[4])

    def y_far(i):
        await_(raw.at[opp_y, i, 0], y_recv.at[i, 2])
        await_(raw.at[opp_y, i, 1], y_recv.at[i, 3])

    def norm(i):
        def step(n, _):
            rows = pl.ds(pl.multiple_of(n * 16, 16), 16)
            squares = jnp.zeros((16, FEAT), jnp.float32)
            crossed = jnp.zeros((16, FEAT), jnp.float32)
            for g in range(4):
                for p in range(2):
                    yval = raw[g, i, p, 0, rows, :].astype(jnp.float32)
                    tval = raw[g, i, p, 1, rows, :].astype(jnp.float32)
                    squares += yval * yval
                    crossed += yval * tval
            rate = lax.rsqrt(jnp.sum(squares, axis=1, keepdims=True) / D + EPS)
            cross = jnp.sum(crossed, axis=1, keepdims=True) / D
            pull = cross * rate * rate
            for g in range(4):
                for p in range(2):
                    yval = raw[g, i, p, 0, rows, :].astype(jnp.float32)
                    tval = raw[g, i, p, 1, rows, :].astype(jnp.float32)
                    scale = gains[g, p, 0:1, :]
                    cols = pl.ds((2 * g + p) * FEAT, FEAT)
                    acts[i, 0, core, rows, cols] = (yval * rate * scale).astype(jnp.bfloat16)
                    acts[i, 1, core, rows, cols] = (scale * rate * (tval - yval * pull)).astype(jnp.bfloat16)
            return 0

        lax.fori_loop(0, SUB // 16, step, 0)

    def send_sibling(i):
        done = acts.at[i, :, core]
        send(done, done, n_send.at[i], n_recv.at[i], sibling)

    def await_sibling(i):
        await_(acts.at[i, :, 1 - core], n_recv.at[i])

    def send_normed(i):
        send(acts.at[i, :, core], acts.at[i + 6, :, core], a_send.at[7 + i], a_recv.at[7 + i], x_to)

    def take_normed(i):
        await_(acts.at[i, :, core], a_recv.at[1 + i])
        send_sibling(i)

    ROWS = 4 * SUB

    def finish(j, i, out):
        gate, upper = out[: ROWS // 2, :UNIT], out[: ROWS // 2, UNIT:]
        gate_t, upper_t = out[ROWS // 2 :, :UNIT], out[ROWS // 2 :, UNIT:]
        sig = jax.nn.sigmoid(gate)
        active = gate * sig
        slope = sig * (1.0 + gate * (1.0 - sig))
        hidden = (active * upper).astype(jnp.bfloat16)
        hidden_tan = (slope * gate_t * upper + active * upper_t).astype(jnp.bfloat16)
        whose = i // 4
        cols = pl.ds(pl.multiple_of(j * UNIT, UNIT), UNIT)
        rows = pl.ds(pl.multiple_of((i + 2 * whose) % 4 * SUB, SUB), SUB)
        for c in range(2):
            results[whose, 0, c, rows, cols] = hidden[c * SUB : (c + 1) * SUB]
            results[whose, 1, c, rows, cols] = hidden_tan[c * SUB : (c + 1) * SUB]

    def multiply(j, i, count):
        lhs, rhs = acts[pl.ds(i, count)].reshape(count * ROWS, D), weights[j].reshape(D, 2 * UNIT)
        out = jnp.dot(lhs, rhs, preferred_element_type=jnp.float32)
        for s in range(count):
            finish(j, i + s, out[s * ROWS : (s + 1) * ROWS])

    def part(j, i, count, step):
        where = (z + step + 4) % 4
        cols = pl.ds(pl.multiple_of(where * (D // 4), D // 4), D // 4)
        lhs = acts[pl.ds(i, count), :, :, :, cols].reshape(count * ROWS, D // 4)
        return jnp.dot(lhs, weights[j, where].reshape(D // 4, 2 * UNIT), preferred_element_type=jnp.float32)

    def multiply_near(j, i, count):
        out = part(j, i, count, 0) + part(j, i, count, -1) + part(j, i, count, 1)
        totals[j % 2, pl.ds(i, count)] = out.reshape(count, ROWS, 2 * UNIT)

    def multiply_far(j, i, count):
        out = totals[j % 2, pl.ds(i, count)].reshape(count * ROWS, 2 * UNIT) + part(j, i, count, 2)
        for s in range(count):
            finish(j, i + s, out[s * ROWS : (s + 1) * ROWS])

    parts = ((0, 2 * UNIT), (2 * UNIT, UNIT), (3 * UNIT, UNIT))

    def give(part, do):
        begin, width = parts[part]
        here = pl.ds(begin, width)
        there = pl.ds(pl.multiple_of(parity * (HID // 2) + begin, UNIT), width)
        for k, out in enumerate((hid_out, hid_tan_out)):
            for c in range(2):
                n = 4 * part + 2 * k + c
                do(n, results.at[1, k, c, :, here], out.at[pl.ds(c * HALF, HALF), there], at_x(1 - 2 * c))

    def give_start(part):
        give(part, lambda n, src, dst, device: send(src, dst, c_send.at[n], c_recv.at[n], device))

    def keep(part):
        begin, width = parts[part]
        there = pl.ds(pl.multiple_of(parity * (HID // 2) + begin, UNIT), width)
        return [
            pltpu.make_async_copy(
                results.at[0, k, c, :, pl.ds(begin, width)], out.at[pl.ds(c * HALF, HALF), there],
                loc.at[24 + 4 * part + 2 * k + c],
            )
            for k, out in enumerate((hid_out, hid_tan_out))
            for c in range(2)
        ]

    def keep_start(part):
        for copy in keep(part):
            copy.start()

    kinds = ("y_far", "y_near", "along_x", "z_near", "z_far", "take", "sibling")
    whole, near, far, whole_pair, near_pair = 0, 1, 2, 3, 4
    plan = (
        (dict(along_x=0), ()),
        (dict(y_near=0), ()),
        (dict(along_x=1), ()),
        (dict(y_far=0, y_near=1, z_near=0), ()),
        (dict(along_x=2), ()),
        (dict(y_far=1, y_near=2, z_near=1), ()),
        (dict(along_x=3), ()),
        (dict(z_far=0, sibling=0), ()),
        (dict(sibling=1), ((whole_pair, 0, (0,)),)),
        (dict(y_far=2, y_near=3), ()),
        (dict(sibling=2), ((whole, 0, (2,)),)),
        (dict(z_near=2, take=6), ((near_pair, 2, (0,)), (near, 2, (2,)))),
        (dict(sibling=6), ((whole, 0, (6,)), (near, 2, (6,)))),
        (dict(y_far=3, y_near=4), ()),
        (dict(z_far=1), ((whole_pair, 1, (0,)), (whole, 1, (2, 6)))),
        (dict(sibling=3), ((whole, 0, (3,)), (whole, 1, (3,)), (near, 2, (3,)))),
        (dict(take=7), ()),
        (dict(y_far=4, y_near=5), ()),
        (dict(sibling=7), ((whole, 0, (7,)), (whole, 1, (7,)), (near, 2, (7,)))),
        (dict(sibling=4), ((whole, 0, (4,)), (whole, 1, (4,)), (near, 2, (4,)))),
        (dict(y_far=5), ()),
        (dict(z_near=3), ((near_pair, 3, (0, 2, 6)),)),
        (dict(sibling=5), ((whole, 0, (5,)), (whole, 1, (5,)))),
        (dict(), ((near, 2, (5,)), (near_pair, 3, (4,)))),
        (dict(z_far=2), ((far, 2, (4, 6, 0)),)),
        (dict(z_far=3), ((far, 3, (4, 6)), (far, 2, (2,)), (far, 3, (0, 2)))),
    )
    slots = [sum((e.get(k, -1) + 1) << 4 * n for n, k in enumerate(kinds)) for e, _ in plan]
    items = [[how << 5 | j << 3 | i for how, j, steps in todo for i in steps] for _, todo in plan]
    codes = [code for todo in items for code in todo]
    bounds = [sum(len(todo) for todo in items[:u]) for u in range(len(items) + 1)]

    def pick(values, n):
        out = jnp.int32(values[0])
        for at in range(1, len(values)):
            if values[at] != values[at - 1]:
                out = jnp.where(n >= at, jnp.int32(values[at]), out)
        return out

    def slot(u, begin):
        code = pick(slots, u)

        def event(kind):
            def run(act):
                index = (lax.shift_right_logical(code, jnp.int32(4 * kinds.index(kind))) & 15) - 1
                pl.when(index >= 0)(lambda: act(index))

            return run

        @event("y_far")
        def _(i):
            y_far(i)
            pl.when(i == 0)(gains_far)
            norm(i)
            send_sibling(i)
            pl.when(i < 2)(lambda: send_normed(i))

        @event("y_near")
        def _(i):
            y_near(i)
            pl.when(i == 0)(gains_near)

            @pl.when(i + 2 < RAW)
            def _():
                pl.when(i >= 2)(lambda: await_(raw.at[y, i + 2], a_recv.at[i + 3]))
                send_y(i + 2)

        @event("along_x")
        def _(j):
            along_x(j)

            @pl.when(j == 0)
            def _():
                send_x(2)
                send_raw()

            pl.when(j == 1)(lambda: send_x(3))

        event("z_near")(z_near)
        event("z_far")(z_far)
        event("take")(take_normed)

        event("sibling")(await_sibling)

        def item(n, _):
            what = pick(codes, n)
            how, j, i = lax.shift_right_logical(what, jnp.int32(5)), lax.shift_right_logical(what, jnp.int32(3)) & 3, what & 7
            pl.when(how == whole)(lambda: multiply(j, i, 1))
            pl.when(how == near)(lambda: multiply_near(j, i, 1))
            pl.when(how == far)(lambda: multiply_far(j, i, 2))
            pl.when(how == whole_pair)(lambda: multiply(j, i, 2))
            pl.when(how == near_pair)(lambda: multiply_near(j, i, 2))
            pl.when(n == bounds[-3] + 1)(lambda: give_start(1))
            pl.when(n == bounds[-2] + 1)(lambda: give_start(2))
            return 0

        end = pick(bounds[1:], u)
        lax.fori_loop(begin, end, item, 0)

        @pl.when(u == len(plan) - 4)
        def _():
            give_start(0)
            keep_start(0)

        return end

    lax.fori_loop(0, len(plan), slot, jnp.int32(0))
    keep_start(1)
    keep_start(2)

    def drain_weights(j, _):
        block, whole_line = weights.at[0, 0, 0], weights.at[0, 0]
        for n in range(3):
            await_(block, w_send.at[j, n])
        for n in (3, 7):
            pl.when(j == last)(lambda: await_(whole_line, w_send.at[j, n]))

            @pl.when(j < last)
            def _():
                for q in range(4):
                    await_(block, w_send.at[j, n + q])

        for n in (11, 12):
            await_(whole_line.at[:, lo], w_send.at[j, n])
        return 0

    lax.fori_loop(0, CHUNKS, drain_weights, 0)

    def drain_raw(i, _):
        block = raw.at[0, 0]
        for n in range(4):
            await_(block if n < 2 else block.at[0], y_send.at[i, n])
        return 0

    lax.fori_loop(0, RAW, drain_raw, 0)

    def drain_normed(i, _):
        await_(acts.at[0, :, 0], n_send.at[i])
        return 0

    lax.fori_loop(0, STEPS, drain_normed, 0)
    for n, ref in enumerate(
        (spare, gain_mine, gain_row, gain_row, gain_row, raw.at[0, 0], raw.at[0, 0], acts.at[0, :, 0], acts.at[0, :, 0])
    ):
        await_(ref, a_send.at[n])
    for part in range(3):
        def leave(n, src, dst, device):
            await_(src, c_send.at[n])
            await_(src, c_recv.at[n])

        give(part, leave)
        for copy in keep(part):
            copy.wait()
    for copy in stores:
        copy.wait()


def settle(*refs):
    ins, outs, held, sems = refs[:4], refs[4:8], refs[8:12], refs[12]
    pieces = [
        (
            pltpu.make_async_copy(ins[n], held[n], sems.at[0, n]),
            pltpu.make_async_copy(held[n], outs[n], sems.at[1, n]),
        )
        for n in range(4)
    ]
    for get, _ in pieces:
        get.start()
    for get, put in pieces:
        get.wait()
        put.start()
    for _, put in pieces:
        put.wait()


def local(resid, attn, attn_tangent, probe, norm_gain, gate_weight, up_weight):
    hbm, vmem = pl.BlockSpec(memory_space=pl.ANY), pl.BlockSpec(memory_space=pltpu.VMEM)
    bf16, f32 = jnp.bfloat16, jnp.float32
    dma = pltpu.SemaphoreType.DMA
    found = pl.pallas_call(
        body,
        name="block",
        out_shape=(
            jax.ShapeDtypeStruct((TOK // SUB, SUB, FEAT), bf16),
            jax.ShapeDtypeStruct((TOK // SUB, SUB, FEAT), bf16),
            jax.ShapeDtypeStruct((TOK, HID), bf16),
            jax.ShapeDtypeStruct((TOK, HID), bf16),
        ),
        in_specs=[hbm, hbm, hbm, hbm, vmem, hbm, hbm],
        out_specs=(hbm, hbm, hbm, hbm),
        scratch_shapes=[
            pltpu.VMEM((CHUNKS, 4, 4, DEPTH, 2 * UNIT), bf16),
            pltpu.VMEM((CHUNKS, DEPTH, 2 * UNIT), bf16),
            pltpu.VMEM((STEPS, 2, 2, SUB, D), bf16),
            pltpu.VMEM((2, STEPS, 4 * SUB, 2 * UNIT), f32),
            pltpu.VMEM((4, RAW, 2, 2, SUB, FEAT), bf16),
            pltpu.VMEM((4, 2, SUB, FEAT), bf16),
            pltpu.VMEM((4, 2, 8, FEAT), f32),
            pltpu.VMEM((2, 2, 2, HALF, HID // 2), bf16),
            pltpu.VMEM((TOK, FEAT), bf16),
            pltpu.VMEM((TOK, FEAT), bf16),
            pltpu.VMEM((TOK, FEAT), bf16),
            pltpu.VMEM((TOK, FEAT), jnp.int32),
            dma((CHUNKS, 13)), dma((CHUNKS, 13)),
            dma((RAW, 4)), dma((RAW, 4)),
            dma((STEPS,)), dma((STEPS,)),
            dma((12,)), dma((12,)),
            dma((9,)), dma((9,)),
            dma((36,)),
        ],
        compiler_params=pltpu.CompilerParams(
            collective_id=0, has_side_effects=True, vmem_limit_bytes=62 << 20
        ),
    )(resid, attn, attn_tangent, probe, norm_gain, gate_weight, up_weight)
    state, state_tan, hidden, hidden_tan = pl.pallas_call(
        settle,
        name="settle",
        out_shape=tuple(jax.ShapeDtypeStruct(a.shape, a.dtype) for a in found),
        in_specs=[hbm] * 4,
        out_specs=(hbm,) * 4,
        scratch_shapes=[*(pltpu.VMEM(a.shape, a.dtype) for a in found), dma((2, 4))],
        compiler_params=pltpu.CompilerParams(vmem_limit_bytes=62 << 20),
    )(*found)
    return state.reshape(TOK, FEAT), state_tan.reshape(TOK, FEAT), hidden, hidden_tan


def solution(mesh):
    in_specs = (
        P("row", "col"),
        P("row", "col"),
        P("row", "col"),
        P("row", "col"),
        P("col"),
        P("row", "col"),
        P("row", "col"),
    )
    out_specs = (P("row", "col"), P("row", "col"), P("row", "col"), P("row", "col"))
    return jax.shard_map(local, mesh=mesh, in_specs=in_specs, out_specs=out_specs, check_vma=False)
```
